128 devices in a mesh: shard: 2 (over z_lo), context: 16 (over x, y), tensor: 4 (over z_hi, core).
Axes of the slice: x: 4, y: 4, z: 4 (z_hi: 2, z_lo: 2; z = z_hi * 2 + z_lo), core: 2. Of those that a mesh axis runs over, the one named last changes fastest.
Arguments:
- tokens: bfloat16 [4, 4096, 960], P('shard', ('context', 'tensor')), may hold values from -6 to 6
- positions: int32 [4, 4096], P('shard', ('context', 'tensor')), may hold values from 0 to 4095, as said below
- out_grad: bfloat16 [4, 4096, 960], P('shard', ('context', 'tensor')), may hold values from -6 to 6
- attn_gain: bfloat16 [960], P(('shard', 'context')), may hold values from 0.099609375 to 1.8984375
- w_query: bfloat16 [960, 960], P(('shard', 'context')), may hold values from -0.1875 to 0.1875
- key_weight: bfloat16 [960, 320], P(('shard', 'context')), may hold values from -0.1875 to 0.1875
- value_weight: bfloat16 [960, 320], P(('shard', 'context')), may hold values from -0.1875 to 0.1875
- w_out: bfloat16 [960, 960], P(('shard', 'context')), may hold values from -1.5 to 1.5
- mlp_gain: bfloat16 [960], P(('shard', 'context')), may hold values from 0.099609375 to 1.8984375
- w_gate: bfloat16 [960, 2560], P(('shard', 'context'), 'tensor'), may hold values from -0.1875 to 0.1875
- w_up: bfloat16 [960, 2560], P(('shard', 'context'), 'tensor'), may hold values from -0.1875 to 0.1875
- w_down: bfloat16 [2560, 960], P('tensor', ('shard', 'context')), may hold values from -0.125 to 0.125
Outputs:
- mixed: bfloat16 [4, 4096, 960], P('shard', ('context', 'tensor'))
- tokens_grad: float32 [4, 4096, 960], P('shard', ('context', 'tensor'))
- attn_gain_grad: float32 [960], P(('shard', 'context'))
- w_query_grad: float32 [960, 960], P(('shard', 'context'))
- w_key_grad: float32 [960, 320], P(('shard', 'context'))
- w_value_grad: float32 [960, 320], P(('shard', 'context'))
- w_out_grad: float32 [960, 960], P(('shard', 'context'))
- mlp_gain_grad: float32 [960], P(('shard', 'context'))
- w_gate_grad: float32 [960, 2560], P(('shard', 'context'), 'tensor')
- w_up_grad: float32 [960, 2560], P(('shard', 'context'), 'tensor')
- w_down_grad: float32 [2560, 960], P('tensor', ('shard', 'context'))
The draws below stay inside these ranges and needn't reach their ends.
Inputs may be any that keep to these rules, and one draw needn't show every extreme that they name: In each sequence the positions count up by one from 0, starting anew at the first token and at the first token of each packed document; at least one sequence is a single document.
All inputs are finite; a program needn't handle non-finite values.
Results may differ from the reference program's by a relative error of at most 0.029.
Values may be sent and summed in bfloat16 or wider, within the bound.
No kernel may reach another device: no remote copies, remote signals or barrier semaphores. Data moves between devices by JAX's collectives and lax.ppermute only.
A program may use at most 128 MiB of HBM per device.

```python
import math
import jax
import jax.numpy as jnp
from jax import lax

MODEL_WIDTH = 960
QUERY_HEADS = 15
KEY_HEADS = 5
HEAD_SIZE = 64
FF = 2560
SEQUENCE_TOKENS = 4096
SEQS = 4


def draw_positions(key, part):
    key = jax.random.fold_in(key, 17)
    start_key, whole_key = jax.random.split(key)
    spacing = max(SEQUENCE_TOKENS // 4, 2)
    starts = jax.random.randint(start_key, (SEQS, SEQUENCE_TOKENS), 0, spacing) == 0
    index = jnp.arange(SEQUENCE_TOKENS, dtype=jnp.int32)
    single = jax.random.randint(whole_key, (), 0, SEQS)
    rows = jnp.arange(SEQS, dtype=jnp.int32)
    starts = starts & (rows[:, None] != single) | (index[None, :] == 0)
    latest = lax.cummax(jnp.where(starts, index[None, :], 0), axis=1)
    return (index[None, :] - latest).astype(jnp.int32)


def steps_of(rng, extent, pieces, least, high):
    loudness = 1.0
    for dim, shards_of in pieces:
        heights = jax.random.uniform(jax.random.fold_in(jax.random.fold_in(rng, 6), dim), (shards_of,), jnp.float32, least / len(pieces), high / len(pieces))
        loudness = loudness * jnp.repeat(jnp.exp(heights), extent[dim] // shards_of).reshape((-1,) + (1,) * (len(extent) - 1 - dim))
    return loudness


def centred(stream_key, shape, scale, limit, pieces=(), kind=jnp.bfloat16):
    drawn = scale * jax.random.normal(stream_key, shape, jnp.float32)
    if pieces:
        drawn = drawn * steps_of(stream_key, shape, pieces, -0.22, 0.18)
    return jnp.clip(drawn, -limit, limit).astype(kind)


def setup_inputs(seed: int = 0) -> dict:
    key_list = jax.random.split(jax.random.key(seed), 13)
    tokens = centred(key_list[0], (SEQS, SEQUENCE_TOKENS, MODEL_WIDTH), 1.0, 6.0, ((0, 2), (1, 64)))
    positions = draw_positions(jax.random.fold_in(key_list[12], 71), 0)
    out_grad = centred(key_list[2], (SEQS, SEQUENCE_TOKENS, MODEL_WIDTH), 1.0, 6.0, ((0, 2), (1, 64)))
    attn_gain = jnp.clip(1.0 + 0.18 * jax.random.normal(key_list[3], (MODEL_WIDTH,), jnp.float32), 0.099609375, 1.8984375).astype(jnp.bfloat16)
    w_query = centred(key_list[4], (MODEL_WIDTH, QUERY_HEADS * HEAD_SIZE), MODEL_WIDTH ** -0.5, 0.1875, ((0, 32),))
    key_weight = centred(key_list[5], (MODEL_WIDTH, KEY_HEADS * HEAD_SIZE), MODEL_WIDTH ** -0.5, 0.1875, ((0, 32),))
    value_weight = centred(key_list[6], (MODEL_WIDTH, KEY_HEADS * HEAD_SIZE), MODEL_WIDTH ** -0.5, 0.1875, ((0, 32),))
    w_out = centred(key_list[7], (QUERY_HEADS * HEAD_SIZE, MODEL_WIDTH), (max(QUERY_HEADS * HEAD_SIZE // 64, 1)) ** -0.5, 1.5, ((0, 32),))
    mlp_gain = jnp.clip(1.0 + 0.18 * jax.random.normal(key_list[8], (MODEL_WIDTH,), jnp.float32), 0.099609375, 1.8984375).astype(jnp.bfloat16)
    w_gate = centred(key_list[9], (MODEL_WIDTH, FF), MODEL_WIDTH ** -0.5, 0.1875, ((0, 32), (1, 4)))
    w_up = centred(key_list[10], (MODEL_WIDTH, FF), MODEL_WIDTH ** -0.5, 0.1875, ((0, 32), (1, 4)))
    w_down = centred(key_list[11], (FF, MODEL_WIDTH), FF ** -0.5, 0.125, ((0, 4), (1, 32)))
    return {"tokens": tokens, "positions": positions, "out_grad": out_grad, "attn_gain": attn_gain, "w_query": w_query, "key_weight": key_weight, "value_weight": value_weight, "w_out": w_out, "mlp_gain": mlp_gain, "w_gate": w_gate, "w_up": w_up, "w_down": w_down}


EPSILON = 1e-05
ROPE_BASE = 100000.0
MASKED = -1e+30
HIGHEST = lax.Precision.HIGHEST

@jax.custom_vjp
def lowered(v):
    return lax.optimization_barrier(v.astype(jnp.bfloat16)).astype(jnp.float32)

@jax.custom_vjp
def lowered_backward(v):
    return v

def low_keep(v):
    return (lowered(v), None)

def low_pass(kept, grad):
    return (grad,)

def back_keep(v):
    return (v, None)

def back_low(kept, grad):
    return (lowered(grad),)
lowered.defvjp(low_keep, low_pass)
lowered_backward.defvjp(back_keep, back_low)

def normalize(value_rows):
    return value_rows * lax.rsqrt(lax.optimization_barrier(jnp.mean(value_rows * value_rows, axis=-1, keepdims=True)) + EPSILON)

def tables(positions, width):
    half = width // 2
    freq = ROPE_BASE ** (-2.0 * jnp.arange(half, dtype=jnp.float32) / width)
    theta = positions.astype(jnp.float32)[..., None] * freq
    return (jnp.cos(theta), jnp.sin(theta))

def apply_rotation(value_rows, cosine_table, sine_table):
    half = value_rows.shape[-1] // 2
    first = value_rows[..., :half]
    second = value_rows[..., half:]
    return jnp.concatenate([first * cosine_table - second * sine_table, second * cosine_table + first * sine_table], axis=-1)

def attend_heads(query_rows, key_rows, value_rows):
    query_block = min(512, SEQUENCE_TOKENS)
    block_list = SEQUENCE_TOKENS // query_block
    head_groups = QUERY_HEADS // KEY_HEADS
    lattice = query_rows.reshape(block_list, query_block, KEY_HEADS, head_groups, HEAD_SIZE)
    starts = jnp.arange(block_list, dtype=jnp.int32) * query_block
    cols = jnp.arange(SEQUENCE_TOKENS, dtype=jnp.int32)
    scale = 1.0 / math.sqrt(HEAD_SIZE)

    def one_block(item):
        part, start = item
        raw = lowered_backward(jnp.einsum('qgrd,kgd->grqk', part, key_rows, precision=HIGHEST))
        rows = start + jnp.arange(query_block, dtype=jnp.int32)
        scores = jnp.where(cols[None, :] <= rows[:, None], raw * scale, MASKED)
        top = lax.optimization_barrier(jnp.max(scores, axis=-1, keepdims=True))
        expo = jnp.exp(scores - top)
        weights = lowered(expo / lax.optimization_barrier(jnp.sum(expo, axis=-1, keepdims=True)))
        return jnp.einsum('grqk,kgd->qgrd', weights, value_rows, precision=HIGHEST)
    result = lax.map(jax.checkpoint(one_block), (lattice, starts))
    return result.reshape(SEQUENCE_TOKENS, QUERY_HEADS * HEAD_SIZE)

def block_layer(resid, cosine_table, sine_table, attn_gain, w_query, key_weight, value_weight, w_out, mlp_gain, w_gate, w_up, w_down):
    hidden_attn = lowered(normalize(resid) * attn_gain)
    query_proj = lowered_backward(jnp.dot(hidden_attn, w_query, precision=HIGHEST, preferred_element_type=jnp.float32))
    key_projected = lowered_backward(jnp.dot(hidden_attn, key_weight, precision=HIGHEST, preferred_element_type=jnp.float32))
    value_lowered = lowered(lowered_backward(jnp.dot(hidden_attn, value_weight, precision=HIGHEST, preferred_element_type=jnp.float32)))
    cosine_heads = cosine_table[:, None, :]
    sine_heads = sine_table[:, None, :]
    query_rows = lowered(apply_rotation(query_proj.reshape(SEQUENCE_TOKENS, QUERY_HEADS, HEAD_SIZE), cosine_heads, sine_heads))
    key_rows = lowered(apply_rotation(key_projected.reshape(SEQUENCE_TOKENS, KEY_HEADS, HEAD_SIZE), cosine_heads, sine_heads))
    attended_rows = lowered(lowered_backward(attend_heads(query_rows, key_rows, value_lowered.reshape(SEQUENCE_TOKENS, KEY_HEADS, HEAD_SIZE))))
    resid_mid = resid + lowered_backward(jnp.dot(attended_rows, w_out, precision=HIGHEST, preferred_element_type=jnp.float32))
    hidden_mlp = lowered(normalize(resid_mid) * mlp_gain)
    gate = lowered_backward(jnp.dot(hidden_mlp, w_gate, precision=HIGHEST, preferred_element_type=jnp.float32))
    upward = lowered_backward(jnp.dot(hidden_mlp, w_up, precision=HIGHEST, preferred_element_type=jnp.float32))
    activated = lowered(jax.nn.silu(gate) * upward)
    return resid_mid + jnp.dot(activated, w_down, precision=HIGHEST, preferred_element_type=jnp.float32)

def reference(tokens, positions, out_grad, attn_gain, w_query, key_weight, value_weight, w_out, mlp_gain, w_gate, w_up, w_down):
    weights = tuple((w.astype(jnp.float32) for w in (attn_gain, w_query, key_weight, value_weight, w_out, mlp_gain, w_gate, w_up, w_down)))

    def step(totals, item):
        inputs, places, cotangent = item
        cosine_table, sine_table = tables(places, HEAD_SIZE)

        def forward(resid, *params):
            return block_layer(resid, cosine_table, sine_table, *params)
        result, pull = jax.vjp(forward, inputs.astype(jnp.float32), *weights)
        grads = pull(cotangent.astype(jnp.float32))
        totals = tuple((a + b for a, b in zip(totals, grads[1:])))
        return (totals, (result.astype(jnp.bfloat16), grads[0]))
    zeros = tuple((jnp.zeros(w.shape, jnp.float32) for w in weights))
    totals, (mixed, tokens_grad) = lax.scan(step, zeros, (tokens, positions, out_grad))
    return (mixed, tokens_grad, totals[0], totals[1], totals[2], totals[3], totals[4], totals[5], totals[6], totals[7], totals[8])
```

```python
import math

import jax
import jax.numpy as jnp
from jax import lax
from jax.experimental import pallas as pl
from jax.experimental.pallas import tpu as pltpu
from jax.sharding import PartitionSpec as P

QH = 15
KH = 5
REP = 3
D = 64
WIDTH = 960
BLK = 30
PADB = 32
NB = 32
WP = NB * PADB
QKV = 1600
FFS = 640
QUART = 448
T = 128
EPSILON = 1e-05
ROPE_BASE = 100000.0
MASKED = -1e30
F32 = jnp.float32
BF16 = jnp.bfloat16
HIGHEST = lax.Precision.HIGHEST
SC = ("shard", "context")
CT = ("context", "tensor")
ALL = ("shard", "context", "tensor")
QB = 8
KB = 512
QN = 256


def dot(a, b, precision=None):
    return lax.dot_general(
        a, b, (((1,), (0,)), ((), ())), precision=precision, preferred_element_type=F32
    )


def dot_t(a, b, precision=None):
    return lax.dot_general(
        a, b, (((1,), (1,)), ((), ())), precision=precision, preferred_element_type=F32
    )


def tdot(a, b):
    return lax.dot_general(a, b, (((0,), (0,)), ((), ())), preferred_element_type=F32)


def call(fn, outs, *args, scratch=(), name=None):
    return pl.pallas_call(
        fn,
        out_shape=tuple(jax.ShapeDtypeStruct(s, d) for s, d in outs),
        scratch_shapes=list(scratch),
        compiler_params=pltpu.CompilerParams(vmem_limit_bytes=56 * 1024 * 1024),
        name=name,
    )(*args)


def exchange(v, axes):
    return lax.all_to_all(v, axes, 0, 0, tiled=True)


def to_all(v, axes):
    n = math.prod(lax.axis_size(a) for a in ((axes,) if isinstance(axes, str) else axes))
    return exchange(jnp.broadcast_to(v, (n, *v.shape)), axes)


def normed(x):
    r = lax.rsqrt(jnp.sum(x * x, axis=-1, keepdims=True) * (1.0 / WIDTH) + EPSILON)
    return x * r, r


def norm_back(m, n, r):
    return r * (m - n * (jnp.sum(m * n, axis=-1, keepdims=True) * (1.0 / WIDTH)))


def turn(x, cos, sin):
    lane = lax.broadcasted_iota(jnp.int32, x.shape, 1)
    partner = jnp.where(
        lax.rem(lane, 64) < 32, pltpu.roll(x, 96, 1), pltpu.roll(x, 32, 1)
    )
    return x * cos + partner * sin


def units():
    for s in range(2):
        for head in range(QH):
            for half in range(2):
                unit = s * 30 + head * 2 + half
                yield unit, s * 64 + half * 32, head * D


def pack_rows(src, send, first):
    for unit, row, col in units():
        send[unit, first : first + 16, :] = jnp.concatenate(
            [src[row : row + 16, col : col + D], src[row + 16 : row + 32, col : col + D]], axis=1
        ).astype(send.dtype)


def unpack_rows(recv, dst, first):
    for unit, row, col in units():
        part = recv[unit, first : first + 16, :].astype(dst.dtype)
        dst[row : row + 16, col : col + D] = part[:, :D]
        dst[row + 16 : row + 32, col : col + D] = part[:, D:]


def pad_kernel(x, dy, e, xp, dyp):
    xp[...] = dot(x[...], e[...]).astype(BF16)
    dyp[...] = dot(dy[...], e[...]).astype(BF16)


def project_kernel(xp, gain, w, cos, sin, send, h1_out, rows):
    n1, _ = normed(xp[...].astype(F32))
    h1 = (n1 * gain[...]).astype(BF16)
    h1_out[...] = h1
    qkv = dot(h1, w[...].reshape(WP, QKV))
    for j in range(10):
        part = turn(qkv[:, 128 * j : 128 * j + 128], cos[...], sin[...])
        lane = lax.broadcasted_iota(jnp.int32, part.shape, 1) + 128 * j
        rows[:, 128 * j : 128 * j + 128] = part
    send[60:64] = jnp.zeros((4, 80, 128), BF16)
    for unit, row, col in units():
        send[unit, 64:80, :] = (
            jnp.concatenate(
                [rows[row : row + 16, col : col + D], rows[row + 16 : row + 32, col : col + D]],
                axis=1,
            ).astype(BF16)
            * 0.125
        ).astype(BF16)
    for s in range(2):
        for g in range(KH):
            both = jnp.concatenate(
                [
                    rows[s * 64 : s * 64 + 64, 960 + D * g : 960 + D * g + D],
                    qkv[s * 64 : s * 64 + 64, 1280 + D * g : 1280 + D * g + D],
                ],
                axis=1,
            ).astype(BF16)
            for u in range(6):
                send[s * 30 + g * 6 + u, 0:64, :] = both


def low_pair(block):
    lane = lax.broadcasted_iota(jnp.int32, block.shape, 1)
    zero = jnp.zeros_like(block)
    return jnp.concatenate(
        [
            jnp.where(lane < D, block, zero),
            jnp.where(lane < D, pltpu.roll(block, D, 1), zero),
        ],
        axis=0,
    ).astype(BF16)


def high_pair(block):
    lane = lax.broadcasted_iota(jnp.int32, block.shape, 1)
    zero = jnp.zeros_like(block)
    return jnp.concatenate(
        [
            jnp.where(lane >= D, pltpu.roll(block, D, 1), zero),
            jnp.where(lane >= D, block, zero),
        ],
        axis=0,
    ).astype(BF16)


def load_pair(ref, qb, first):
    return ref[pl.ds(qb * 8, 8), first : first + 16, :].reshape(T, 128).astype(F32)


def unpair(cols):
    flat = cols.T
    return jnp.concatenate([flat[:T], flat[T:]], axis=1).astype(BF16).reshape(8, 16, 128)


def attend_kernel(recv, qpos, send, o_out, lse_out, kv_t, scores):
    for kb in range(QB):
        block = recv[kb * 8 : kb * 8 + 8, 0:64, :].reshape(KB, 128)
        kv_t[kb] = block.astype(F32).T.astype(BF16)

    def key_block(kb):
        return recv[pl.ds(kb * 8, 8), 0:64, :].reshape(KB, 128)

    def one(qb, carry):
        q = low_pair(load_pair(recv, qb, 64))

        def first(kb, top):
            raw = dot_t(key_block(kb), q)
            scores[kb] = raw
            return jnp.maximum(top, jnp.max(raw.reshape(KB // 8, 8, QN), axis=0))

        top = lax.fori_loop(0, qb, first, jnp.full((8, QN), MASKED, F32))
        raw = dot_t(key_block(qb), q)
        kpos = lax.broadcasted_iota(jnp.int32, (KB, QN), 0)
        raw = jnp.where(kpos <= qpos[...], raw, MASKED)
        scores[qb] = raw
        top = jnp.maximum(top, jnp.max(raw.reshape(KB // 8, 8, QN), axis=0))
        top = jnp.max(top, axis=0, keepdims=True)

        def second(kb, carry):
            mass, acc = carry
            p = jnp.exp(scores[kb] - top)
            mass = mass + jnp.sum(p.reshape(KB // 8, 8, QN), axis=0)
            acc = acc + dot(kv_t[kb, D:, :], p.astype(BF16))
            return mass, acc

        mass, acc = lax.fori_loop(
            0, qb + 1, second, (jnp.zeros((8, QN), F32), jnp.zeros((D, QN), F32))
        )
        mass = jnp.sum(mass, axis=0, keepdims=True)
        acc = acc / mass
        o_out[qb] = acc
        lse_out[qb] = jnp.broadcast_to(top + jnp.log(mass), (8, QN))
        send[pl.ds(qb * 8, 8)] = unpair(acc)
        return carry

    lax.fori_loop(0, QB, one, 0)


def attend_back_kernel(recv, qpos, drecv, o_in, lse_in, send, kv_t, dkv):
    for kb in range(QB):
        block = recv[kb * 8 : kb * 8 + 8, 0:64, :].reshape(KB, 128)
        kv_t[kb] = block[:, :D].astype(F32).T.astype(BF16)
    dkv[...] = jnp.zeros_like(dkv)

    def one(qb, carry):
        q = low_pair(load_pair(recv, qb, 64))
        pair = load_pair(drecv, qb, 0)
        dz = high_pair(pair)
        flat = jnp.concatenate([pair[:, :D], pair[:, D:]], axis=0)
        delta = jnp.sum(flat.T * o_in[qb], axis=0, keepdims=True)
        lse = lse_in[qb][0:1]

        def tile(kb, acc, diagonal):
            block = recv[pl.ds(kb * 8, 8), 0:64, :].reshape(KB, 128)
            raw = dot_t(block, q)
            if diagonal:
                kpos = lax.broadcasted_iota(jnp.int32, (KB, QN), 0)
                raw = jnp.where(kpos <= qpos[...], raw, MASKED)
            p = jnp.exp(raw - lse)
            ds = (p * (dot_t(block, dz) - delta)).astype(BF16)
            dkv[kb] += dot(ds, q) + dot(p.astype(BF16), dz)
            return acc + dot(kv_t[kb], ds)

        acc = lax.fori_loop(0, qb, lambda kb, a: tile(kb, a, False), jnp.zeros((D, QN), F32))
        acc = tile(qb, acc, True)
        send[pl.ds(qb * 8, 8), 64:80, :] = unpair(acc * 0.125)
        return carry

    lax.fori_loop(0, QB, one, 0)
    for kb in range(QB):
        send[kb * 8 : kb * 8 + 8, 0:64, :] = dkv[kb].astype(BF16).reshape(8, 64, 128)


def out_kernel(recv, xp, e, gain, w, olp_out, x1_out, h2_out, ol):
    unpack_rows(recv, ol, 0)
    olp = dot(ol[...], e[...]).astype(BF16)
    olp_out[...] = olp
    x1 = xp[...].astype(F32) + dot(olp, w[...].reshape(WP, WP))
    x1_out[...] = x1
    n2, _ = normed(x1)
    h2_out[...] = (n2 * gain[...]).astype(BF16)


def mlp_kernel(h2, dy, w, part, dh2, act, dgate, dup):
    wg = w[:, 0:32, :].reshape(WP, FFS)
    wu = w[:, 32:64, :].reshape(WP, FFS)
    wd = w[:, 64:96, :].reshape(WP, FFS)
    for i in range(4):
        h = h2[i]
        gate = dot(h, wg)
        up = dot(h, wu)
        sig = jax.nn.sigmoid(gate)
        silu = gate * sig
        a = (silu * up).astype(BF16)
        act[i] = a
        part[i] = dot_t(a, wd).astype(BF16)
        dact = dot(dy[i], wd)
        dg = (dact * up * sig * (1.0 + gate * (1.0 - sig))).astype(BF16)
        du = (dact * silu).astype(BF16)
        dgate[i] = dg
        dup[i] = du
        dh2[i] = (dot_t(dg, wg) + dot_t(du, wu)).astype(BF16)


def mlp_grad_kernel(h2, dy, act, dgate, dup, out):
    h = h2[...].reshape(4 * T, WP)
    out[:, 0:32, :] = tdot(h, dgate[...].reshape(4 * T, FFS)).astype(BF16).reshape(NB, 32, FFS)
    out[:, 32:64, :] = tdot(h, dup[...].reshape(4 * T, FFS)).astype(BF16).reshape(NB, 32, FFS)
    d = dy[...].reshape(4 * T, WP)
    out[:, 64:96, :] = tdot(d, act[...].reshape(4 * T, FFS)).astype(BF16).reshape(NB, 32, FFS)


def mixed_kernel(parts, x1, e, out):
    total = jnp.sum(parts[...].astype(F32), axis=0)
    out[...] = dot_t((x1[...] + total).astype(BF16), e[...]).astype(BF16)


def mid_back_kernel(parts, x1, gain, dyp, w, e, dx1_out, da_out, send, gain_part, dol):
    dh2 = jnp.sum(parts[...].astype(F32), axis=0)
    n2, r2 = normed(x1[...])
    gain_part[...] = jnp.sum(dh2 * n2, axis=0, keepdims=True)
    dx1 = dyp[...].astype(F32) + norm_back(dh2 * gain[...], n2, r2)
    dx1_out[...] = dx1
    da = dx1.astype(BF16)
    da_out[...] = da
    wide = dot_t(da, w[...].reshape(WP, WP)).astype(BF16)
    dol[...] = dot_t(wide, e[...]).astype(BF16)
    send[60:64] = jnp.zeros((4, 16, 128), BF16)
    pack_rows(dol, send, 0)


def out_grad_kernel(olp, da, out):
    for t in range(4):
        out[:, t] = (
            tdot(olp[...], da[:, 256 * t : 256 * t + 256]).astype(BF16).reshape(NB, 32, 256)
        )


def unpack_back_kernel(recv, cos, sin, full, send, rows):
    unpack_rows(recv, rows, 64)
    full[:, QKV:] = jnp.zeros((T, 4 * QUART - QKV), BF16)
    for s in range(2):
        for g in range(KH):
            total = recv[s * 30 + g * 6, 0:64, :].astype(F32)
            for u in range(1, 6):
                total = total + recv[s * 30 + g * 6 + u, 0:64, :].astype(F32)
            rows[s * 64 : s * 64 + 64, 960 + D * g : 960 + D * g + D] = total[:, :D]
            full[s * 64 : s * 64 + 64, 1280 + D * g : 1280 + D * g + D] = total[:, D:].astype(BF16)
    for j in range(10):
        full[:, 128 * j : 128 * j + 128] = turn(
            rows[:, 128 * j : 128 * j + 128], cos[...], -sin[...]
        ).astype(BF16)
    for t in range(4):
        send[t] = full[:, QUART * t : QUART * t + QUART]


def tokens_back_kernel(full, w, xp, gain, dx1, e, tokens_grad, gain_part):
    dh1 = dot_t(full[:, :QKV], w[...].reshape(WP, QKV))
    n1, r1 = normed(xp[...].astype(F32))
    gain_part[...] = jnp.sum(dh1 * n1, axis=0, keepdims=True)
    grad = dx1[...] + norm_back(dh1 * gain[...], n1, r1)
    tokens_grad[...] = dot_t(grad, e[...].astype(F32), HIGHEST)


def proj_grad_kernel(h1, dq, gains, out):
    out[...] = (
        tdot(h1[...].reshape(4 * T, WP), dq[...].reshape(4 * T, QUART))
        .astype(BF16)
        .reshape(NB, 32, QUART)
    )
    out[:, 30:31, :] = gains[...]


def pad_rows(w, extra=None):
    rows = [w]
    if extra is not None:
        rows.append(jnp.pad(extra[None, :], ((0, 0), (0, w.shape[1] - extra.shape[0]))))
    rows.append(jnp.zeros((PADB - BLK - (extra is not None), w.shape[1]), w.dtype))
    return jnp.concatenate(rows, axis=0)


def shards(
    tokens,
    positions,
    out_grad,
    attn_gain,
    w_query,
    key_weight,
    value_weight,
    w_out,
    mlp_gain,
    w_gate,
    w_up,
    w_down,
):
    i = lax.broadcasted_iota(jnp.int32, (WIDTH, WP), 0)
    j = lax.broadcasted_iota(jnp.int32, (WIDTH, WP), 1)
    spread = (j == (i // BLK) * PADB + i % BLK).astype(BF16)

    w1 = to_all(pad_rows(jnp.concatenate([w_query, key_weight, value_weight], axis=1), attn_gain), SC)
    gain1 = w1[:, 30, :PADB].reshape(1, WP).astype(F32)

    own_out = jnp.dot(w_out, spread, preferred_element_type=F32).astype(BF16)
    own_mlp = jnp.concatenate(
        [pad_rows(w_gate, mlp_gain), pad_rows(w_up), pad_rows(w_down.T)], axis=0
    )
    own_out, own_mlp, w1 = lax.optimization_barrier((own_out, own_mlp, w1))
    w2 = to_all(pad_rows(own_out), SC)
    w3 = to_all(own_mlp, SC)
    gain2 = w3[:, 30, :PADB].reshape(1, WP).astype(F32)

    half = D // 2
    freq = ROPE_BASE ** (-2.0 * jnp.arange(half, dtype=F32) / D)
    theta = positions.reshape(T).astype(F32)[:, None] * freq
    c, s = jnp.cos(theta), jnp.sin(theta)
    cos = jnp.concatenate([c, c, c, c], axis=1)
    sin = jnp.concatenate([-s, s, -s, s], axis=1)

    xp, dyp = call(
        pad_kernel,
        [((T, WP), BF16), ((T, WP), BF16)],
        tokens.reshape(T, WIDTH),
        out_grad.reshape(T, WIDTH),
        spread,
    )
    dy_all = to_all(dyp, "tensor").reshape(4, T, WP)

    send, h1 = call(
        project_kernel,
        [((64, 80, 128), BF16), ((T, WP), BF16)],
        xp, gain1, w1, cos, sin,
        scratch=[pltpu.VMEM((T, 1280), F32)],
    )
    recv = exchange(send, CT)
    h1_all = to_all(h1, "tensor").reshape(4, T, WP)

    lane = jnp.arange(QN, dtype=jnp.int32)
    qpos = (
        64 * ((lane % T) // 16)
        + 32 * (lax.axis_index("tensor") % 2)
        + 16 * (lane // T)
        + lane % 16
    ).reshape(1, QN)
    o_send, o_cols, lse = call(
        attend_kernel,
        [((64, 16, 128), BF16), ((QB, D, QN), F32), ((QB, 8, QN), F32)],
        recv, qpos,
        scratch=[pltpu.VMEM((QB, 128, KB), BF16), pltpu.VMEM((QB, KB, QN), F32)],
    )
    o_recv = exchange(o_send, CT)

    olp, x1, h2 = call(
        out_kernel,
        [((T, WP), BF16), ((T, WP), F32), ((T, WP), BF16)],
        o_recv, xp, spread, gain2, w2,
        scratch=[pltpu.VMEM((T, WIDTH), BF16)],
    )
    h2_all = to_all(h2, "tensor").reshape(4, T, WP)

    part, dh2_part, act, dgate, dup = call(
        mlp_kernel,
        [((4, T, WP), BF16), ((4, T, WP), BF16)] + [((4, T, FFS), BF16)] * 3,
        h2_all, dy_all, w3,
    )
    dh2_recv = exchange(dh2_part, "tensor")
    (mlp_grad,) = call(
        mlp_grad_kernel, [((NB, 96, FFS), BF16)], h2_all, dy_all, act, dgate, dup
    )

    dx1, da, d_send, gain2_part = call(
        mid_back_kernel,
        [((T, WP), F32), ((T, WP), BF16), ((64, 16, 128), BF16), ((1, WP), F32)],
        dh2_recv, x1, gain2, dyp, w2, spread,
        scratch=[pltpu.VMEM((T, WIDTH), BF16)],
    )
    d_recv = exchange(d_send, CT)
    part_recv = exchange(part, "tensor")
    mlp_recv = exchange(mlp_grad, SC)

    (mixed,) = call(mixed_kernel, [((T, WIDTH), BF16)], part_recv, x1, spread)
    (out_w_grad,) = call(out_grad_kernel, [((NB, 4, 32, 256), BF16)], olp, da)
    out_recv = exchange(out_w_grad.reshape(NB * 4, 32, 256), ALL)

    (back_send,) = call(
        attend_back_kernel,
        [((64, 80, 128), BF16)],
        recv, qpos, d_recv, o_cols, lse,
        scratch=[pltpu.VMEM((QB, D, KB), BF16), pltpu.VMEM((QB, KB, 128), F32)],
    )
    back_recv = exchange(back_send, CT)

    full, dq_send = call(
        unpack_back_kernel,
        [((T, 4 * QUART), BF16), ((4, T, QUART), BF16)],
        back_recv, cos, sin,
        scratch=[pltpu.VMEM((T, 1280), F32)],
    )
    dq_recv = exchange(dq_send, "tensor")
    tokens_grad, gain1_part = call(
        tokens_back_kernel,
        [((T, WIDTH), F32), ((1, WP), F32)],
        full, w1, xp, gain1, dx1, spread,
    )
    gains = jnp.concatenate(
        [gain1_part.reshape(NB, PADB), gain2_part.reshape(NB, PADB)], axis=1
    ).astype(BF16)
    gains = jnp.pad(gains, ((0, 0), (0, QUART - 2 * PADB))).reshape(NB, 1, QUART)
    (proj_grad,) = call(
        proj_grad_kernel, [((NB, 32, QUART), BF16)], h1_all, dq_recv, gains
    )
    proj_sum = jnp.sum(exchange(proj_grad, SC).astype(F32), axis=0)

    mlp_sum = jnp.sum(mlp_recv.astype(F32), axis=0)
    out_sum = jnp.sum(out_recv.astype(F32), axis=0)
    out_all = to_all(out_sum.astype(BF16), "tensor")
    out_all = jnp.moveaxis(out_all, 0, 1).reshape(32, WP)[:BLK].astype(BF16)
    wout_grad = jnp.einsum("rp,dp->rd", out_all, spread, preferred_element_type=F32)

    proj_all = to_all(proj_sum.astype(BF16), "tensor").astype(F32)
    gain_sums = jnp.sum(proj_all[:, 30, : 2 * PADB], axis=0)
    proj_full = jnp.moveaxis(proj_all[:, :BLK], 0, 1).reshape(BLK, 4 * QUART)
    return (
        mixed.reshape(tokens.shape),
        tokens_grad.reshape(tokens.shape),
        gain_sums[:BLK],
        proj_full[:, :960],
        proj_full[:, 960:1280],
        proj_full[:, 1280:1600],
        wout_grad,
        gain_sums[PADB : PADB + BLK],
        mlp_sum[:BLK],
        mlp_sum[32 : 32 + BLK],
        mlp_sum[64 : 64 + BLK].T,
    )


def solution(mesh):
    tok = P("shard", ("context", "tensor"), None)
    vec = P(SC)
    row = P(SC, None)
    wide = P(SC, "tensor")
    return jax.shard_map(
        shards,
        mesh=mesh,
        in_specs=(
            tok, P("shard", ("context", "tensor")), tok,
            vec, row, row, row, row, vec, wide, wide, P("tensor", SC),
        ),
        out_specs=(
            tok, tok, vec, row, row, row, row, vec, wide, wide, P("tensor", SC),
        ),
        check_vma=False,
    )
```

```python
import math

import jax
import jax.numpy as jnp
from jax import lax
from jax.experimental import pallas as pl
from jax.experimental.pallas import tpu as pltpu
from jax.sharding import PartitionSpec as P

QH = 15
KH = 5
REP = 3
D = 64
WIDTH = 960
BLK = 30
PADB = 32
NB = 32
WP = NB * PADB
QKV = 1600
FFS = 640
QUART = 640
HALF = 832
T = 128
EPSILON = 1e-05
ROPE_BASE = 100000.0
MASKED = -1e30
F32 = jnp.float32
BF16 = jnp.bfloat16
HIGHEST = lax.Precision.HIGHEST
SC = ("shard", "context")
CS = ("context", "shard")
CT = ("context", "tensor")
ALL = ("shard", "context", "tensor")
QB = 8
KB = 512
QN = 256


def dot(a, b, precision=None):
    return lax.dot_general(
        a, b, (((1,), (0,)), ((), ())), precision=precision, preferred_element_type=F32
    )


def dot_t(a, b, precision=None):
    return lax.dot_general(
        a, b, (((1,), (1,)), ((), ())), precision=precision, preferred_element_type=F32
    )


def tdot(a, b):
    return lax.dot_general(a, b, (((0,), (0,)), ((), ())), preferred_element_type=F32)


def call(fn, outs, *args, scratch=(), specs=None):
    whole = pl.BlockSpec(memory_space=pltpu.VMEM)
    return pl.pallas_call(
        fn,
        in_specs=[(specs or {}).get(k, whole) for k in range(len(args))],
        out_specs=tuple(whole for _ in outs),
        out_shape=tuple(jax.ShapeDtypeStruct(s, d) for s, d in outs),
        scratch_shapes=list(scratch),
        compiler_params=pltpu.CompilerParams(vmem_limit_bytes=56 * 1024 * 1024),
    )(*args)


def exchange(v, axes):
    return lax.all_to_all(v, axes, 0, 0, tiled=True)


def to_all(v, axes):
    n = math.prod(lax.axis_size(a) for a in ((axes,) if isinstance(axes, str) else axes))
    return exchange(jnp.broadcast_to(v, (n, *v.shape)), axes)


def swap(v, axis, bit):
    pairs = [(i, i ^ bit) for i in range(lax.axis_size(axis))]
    return lax.ppermute(v, axis, pairs)


def from_tensor(v):
    near = jnp.stack([v, swap(v, "tensor", 2)])
    return near, swap(near, "tensor", 1)


def gathered(v):
    mine = lax.axis_index("shard") == 0
    other = swap(v, "shard", 1)
    pair = jnp.concatenate([jnp.where(mine, v, other), jnp.where(mine, other, v)], axis=0)
    return lax.all_gather(pair, "context", axis=0, tiled=True).reshape(NB, *v.shape)


def scattered(v):
    n = v.shape[1]
    flat = v.reshape(NB * n, v.shape[2])
    part = lax.psum_scatter(flat, "context", scatter_dimension=0, tiled=True)
    mine = lax.axis_index("shard") == 0
    keep = jnp.where(mine, part[:n], part[n:])
    away = jnp.where(mine, part[n:], part[:n])
    return keep.astype(F32) + swap(away, "shard", 1).astype(F32)


def normed(x):
    r = lax.rsqrt(jnp.sum(x * x, axis=-1, keepdims=True) * (1.0 / WIDTH) + EPSILON)
    return x * r, r


def norm_back(m, n, r):
    return r * (m - n * (jnp.sum(m * n, axis=-1, keepdims=True) * (1.0 / WIDTH)))


def turn(x, cos, sin):
    lane = lax.broadcasted_iota(jnp.int32, x.shape, 1)
    partner = jnp.where(
        lax.rem(lane, 64) < 32, pltpu.roll(x, 96, 1), pltpu.roll(x, 32, 1)
    )
    return x * cos + partner * sin


def units():
    for s in range(2):
        for head in range(QH):
            for half in range(2):
                unit = s * 30 + head * 2 + half
                yield unit, s * 64 + half * 32, head * D


def pack_rows(src, send, first):
    for unit, row, col in units():
        send[unit, first : first + 16, :] = jnp.concatenate(
            [src[row : row + 16, col : col + D], src[row + 16 : row + 32, col : col + D]], axis=1
        ).astype(send.dtype)


def unpack_rows(recv, dst, first):
    for unit, row, col in units():
        part = recv[unit, first : first + 16, :].astype(dst.dtype)
        dst[row : row + 16, col : col + D] = part[:, :D]
        dst[row + 16 : row + 32, col : col + D] = part[:, D:]


def first_kernel(wq, wk, wv, gain, core, out):
    zero = jnp.zeros((BLK, 64), BF16)
    low = wq[:, :HALF]
    high = jnp.concatenate([wq[:, HALF:], wk[...], wv[...], zero], axis=1)
    half = jnp.where(core[...] == 0, low.astype(F32), high.astype(F32)).astype(BF16)
    tail = jnp.concatenate([gain[...], jnp.zeros((1, HALF), BF16)], axis=0)
    block = jnp.concatenate([half, tail], axis=0)
    for b in range(NB):
        out[b] = block


def shard_kernel(wg, wu, wd, wo, gain, e, mlp, out):
    zero = jnp.zeros((2, FFS), BF16)
    i = lax.broadcasted_iota(jnp.int32, (PADB, BLK), 0)
    j = lax.broadcasted_iota(jnp.int32, (PADB, BLK), 1)
    eye = (i == j).astype(F32).astype(BF16)
    mlp[0:32, :] = dot(eye, wg[...]).astype(BF16)
    mlp[30:31, :] = gain[...]
    mlp[32:64, :] = dot(eye, wu[...]).astype(BF16)
    mlp[64:96, :] = dot_t(eye, wd[...]).astype(BF16)
    out[...] = dot(eye, dot(wo[...], e[...]).astype(BF16)).astype(BF16)


def pad_kernel(x, dy, e, xp, dyp):
    xp[...] = dot(x[...], e[...]).astype(BF16)
    dyp[...] = dot(dy[...], e[...]).astype(BF16)


def project_kernel(xp, gain, wa, wb, core, cos, sin, send, h1_out, rows):
    n1, _ = normed(xp[...].astype(F32))
    h1 = (n1 * gain[...]).astype(BF16)
    h1_out[...] = h1
    ya = dot(h1, wa[...].reshape(WP, HALF))
    yb = dot(h1, wb[...].reshape(WP, HALF))
    first = core[...] == 0
    low = jnp.where(first, ya, yb)
    high = jnp.where(first, yb, ya)
    qkv = jnp.concatenate([low, high[:, : QKV - HALF]], axis=1)
    for j in range(10):
        part = turn(qkv[:, 128 * j : 128 * j + 128], cos[...], sin[...])
        rows[:, 128 * j : 128 * j + 128] = part
    send[60:64] = jnp.zeros((4, 80, 128), BF16)
    for unit, row, col in units():
        send[unit, 64:80, :] = (
            jnp.concatenate(
                [rows[row : row + 16, col : col + D], rows[row + 16 : row + 32, col : col + D]],
                axis=1,
            ).astype(BF16)
            * 0.125
        ).astype(BF16)
    for s in range(2):
        for g in range(KH):
            both = jnp.concatenate(
                [
                    rows[s * 64 : s * 64 + 64, 960 + D * g : 960 + D * g + D],
                    qkv[s * 64 : s * 64 + 64, 1280 + D * g : 1280 + D * g + D],
                ],
                axis=1,
            ).astype(BF16)
            for u in range(6):
                send[s * 30 + g * 6 + u, 0:64, :] = both


def low_pair(block):
    lane = lax.broadcasted_iota(jnp.int32, block.shape, 1)
    zero = jnp.zeros_like(block)
    return jnp.concatenate(
        [
            jnp.where(lane < D, block, zero),
            jnp.where(lane < D, pltpu.roll(block, D, 1), zero),
        ],
        axis=0,
    ).astype(BF16)


def high_pair(block):
    lane = lax.broadcasted_iota(jnp.int32, block.shape, 1)
    zero = jnp.zeros_like(block)
    return jnp.concatenate(
        [
            jnp.where(lane >= D, pltpu.roll(block, D, 1), zero),
            jnp.where(lane >= D, block, zero),
        ],
        axis=0,
    ).astype(BF16)


def load_pair(ref, qb, first):
    return ref[pl.ds(qb * 8, 8), first : first + 16, :].reshape(T, 128).astype(F32)


def unpair(cols):
    flat = cols.T
    return jnp.concatenate([flat[:T], flat[T:]], axis=1).astype(BF16).reshape(8, 16, 128)


def attend_kernel(recv, qpos, send, o_out, lse_out, kv_t, scores):
    for kb in range(QB):
        block = recv[kb * 8 : kb * 8 + 8, 0:64, :].reshape(KB, 128)
        kv_t[kb] = block.astype(F32).T.astype(BF16)

    def key_block(kb):
        return recv[pl.ds(kb * 8, 8), 0:64, :].reshape(KB, 128)

    def one(qb, carry):
        q = low_pair(load_pair(recv, qb, 64))

        def first(kb, top):
            raw = dot_t(key_block(kb), q)
            scores[kb] = raw
            return jnp.maximum(top, jnp.max(raw.reshape(KB // 8, 8, QN), axis=0))

        top = lax.fori_loop(0, qb, first, jnp.full((8, QN), MASKED, F32))
        raw = dot_t(key_block(qb), q)
        kpos = lax.broadcasted_iota(jnp.int32, (KB, QN), 0)
        raw = jnp.where(kpos <= qpos[...], raw, MASKED)
        scores[qb] = raw
        top = jnp.maximum(top, jnp.max(raw.reshape(KB // 8, 8, QN), axis=0))
        top = jnp.max(top, axis=0, keepdims=True)

        def second(kb, carry):
            mass, acc = carry
            p = jnp.exp(scores[kb] - top)
            mass = mass + jnp.sum(p.reshape(KB // 8, 8, QN), axis=0)
            acc = acc + dot(kv_t[kb, D:, :], p.astype(BF16))
            return mass, acc

        mass, acc = lax.fori_loop(
            0, qb + 1, second, (jnp.zeros((8, QN), F32), jnp.zeros((D, QN), F32))
        )
        mass = jnp.sum(mass, axis=0, keepdims=True)
        acc = acc / mass
        o_out[qb] = acc
        lse_out[qb] = jnp.broadcast_to(top + jnp.log(mass), (8, QN))
        send[pl.ds(qb * 8, 8)] = unpair(acc)
        return carry

    lax.fori_loop(0, QB, one, 0)


def attend_back_kernel(recv, qpos, drecv, o_in, lse_in, send, kv_t, dkv):
    for kb in range(QB):
        block = recv[kb * 8 : kb * 8 + 8, 0:64, :].reshape(KB, 128)
        kv_t[kb] = block[:, :D].astype(F32).T.astype(BF16)
    dkv[...] = jnp.zeros_like(dkv)

    def one(qb, carry):
        q = low_pair(load_pair(recv, qb, 64))
        pair = load_pair(drecv, qb, 0)
        dz = high_pair(pair)
        flat = jnp.concatenate([pair[:, :D], pair[:, D:]], axis=0)
        delta = jnp.sum(flat.T * o_in[qb], axis=0, keepdims=True)
        lse = lse_in[qb][0:1]

        def tile(kb, acc, diagonal):
            block = recv[pl.ds(kb * 8, 8), 0:64, :].reshape(KB, 128)
            raw = dot_t(block, q)
            if diagonal:
                kpos = lax.broadcasted_iota(jnp.int32, (KB, QN), 0)
                raw = jnp.where(kpos <= qpos[...], raw, MASKED)
            p = jnp.exp(raw - lse)
            ds = (p * (dot_t(block, dz) - delta)).astype(BF16)
            dkv[kb] += dot(ds, q) + dot(p.astype(BF16), dz)
            return acc + dot(kv_t[kb], ds)

        acc = lax.fori_loop(0, qb, lambda kb, a: tile(kb, a, False), jnp.zeros((D, QN), F32))
        acc = tile(qb, acc, True)
        send[pl.ds(qb * 8, 8), 64:80, :] = unpair(acc * 0.125)
        return carry

    lax.fori_loop(0, QB, one, 0)
    for kb in range(QB):
        send[kb * 8 : kb * 8 + 8, 0:64, :] = dkv[kb].astype(BF16).reshape(8, 64, 128)


def out_kernel(recv, xp, e, gain, w, olp_out, x1_out, h2_out, ol):
    unpack_rows(recv, ol, 0)
    olp = dot(ol[...], e[...]).astype(BF16)
    olp_out[...] = olp
    x1 = xp[...].astype(F32) + dot(olp, w[...].reshape(WP, WP))
    x1_out[...] = x1
    n2, _ = normed(x1)
    h2_out[...] = (n2 * gain[...]).astype(BF16)


def mlp_kernel(near, far, dnear, dfar, w, part, part_far, dh2, dh2_far, act, dgate, dup):
    wg = w[:, 0:32, :].reshape(WP, FFS)
    wu = w[:, 32:64, :].reshape(WP, FFS)
    wd = w[:, 64:96, :].reshape(WP, FFS)
    for i in range(4):
        h = near[i] if i < 2 else far[i - 2]
        dy = dnear[i] if i < 2 else dfar[i - 2]
        gate = dot(h, wg)
        up = dot(h, wu)
        sig = jax.nn.sigmoid(gate)
        silu = gate * sig
        a = (silu * up).astype(BF16)
        act[i] = a
        y = dot_t(a, wd).astype(BF16)
        dact = dot(dy, wd)
        dg = (dact * up * sig * (1.0 + gate * (1.0 - sig))).astype(BF16)
        du = (dact * silu).astype(BF16)
        dgate[i] = dg
        dup[i] = du
        back = (dot_t(dg, wg) + dot_t(du, wu)).astype(BF16)
        if i < 2:
            part[i] = y
            dh2[i] = back
        else:
            part_far[i - 2] = y
            dh2_far[i - 2] = back


def mlp_grad_kernel(near, far, dnear, dfar, act, dgate, dup, out):
    h = jnp.concatenate([near[...].reshape(2 * T, WP), far[...].reshape(2 * T, WP)], axis=0)
    d = jnp.concatenate([dnear[...].reshape(2 * T, WP), dfar[...].reshape(2 * T, WP)], axis=0)
    out[:, 0:32, :] = tdot(h, dgate[...].reshape(4 * T, FFS)).astype(BF16).reshape(NB, 32, FFS)
    out[:, 32:64, :] = tdot(h, dup[...].reshape(4 * T, FFS)).astype(BF16).reshape(NB, 32, FFS)
    out[:, 64:96, :] = tdot(d, act[...].reshape(4 * T, FFS)).astype(BF16).reshape(NB, 32, FFS)


def mixed_kernel(own, away, x1, e, out):
    total = own[0].astype(F32) + away[...].astype(F32)
    out[...] = dot_t((x1[...] + total).astype(BF16), e[...]).astype(BF16)


def mid_back_kernel(own, away, x1, gain, dyp, w, e, dx1_out, da_out, send, gain_part, dol):
    dh2 = own[0].astype(F32) + away[...].astype(F32)
    n2, r2 = normed(x1[...])
    gain_part[...] = jnp.sum(dh2 * n2, axis=0, keepdims=True)
    dx1 = dyp[...].astype(F32) + norm_back(dh2 * gain[...], n2, r2)
    dx1_out[...] = dx1
    da = dx1.astype(BF16)
    da_out[...] = dot_t(da, e[...]).astype(BF16)
    wide = dot_t(da, w[...].reshape(WP, WP)).astype(BF16)
    dol[...] = dot_t(wide, e[...]).astype(BF16)
    send[60:64] = jnp.zeros((4, 16, 128), BF16)
    pack_rows(dol, send, 0)


def unpack_back_kernel(recv, cos, sin, da, full, send, rows):
    unpack_rows(recv, rows, 64)
    for s in range(2):
        for g in range(KH):
            total = recv[s * 30 + g * 6, 0:64, :].astype(F32)
            for u in range(1, 6):
                total = total + recv[s * 30 + g * 6 + u, 0:64, :].astype(F32)
            rows[s * 64 : s * 64 + 64, 960 + D * g : 960 + D * g + D] = total[:, :D]
            full[s * 64 : s * 64 + 64, 1280 + D * g : 1280 + D * g + D] = total[:, D:].astype(BF16)
    for j in range(10):
        full[:, 128 * j : 128 * j + 128] = turn(
            rows[:, 128 * j : 128 * j + 128], cos[...], -sin[...]
        ).astype(BF16)
    for t in range(4):
        first = QUART * t
        inside = min(max(QKV - first, 0), QUART)
        if inside:
            send[t, :, :inside] = full[:, first : first + inside]
        if inside < QUART:
            start = first + inside - QKV
            send[t, :, inside:] = da[:, start : start + QUART - inside]


def tokens_back_kernel(full, wa, wb, core, xp, gain, dx1, e, tokens_grad, gain_part):
    low = full[:, :HALF].astype(F32)
    high = jnp.concatenate([full[:, HALF:], jnp.zeros((T, 64), BF16)], axis=1).astype(F32)
    first = core[...] == 0
    ga = jnp.where(first, low, high).astype(BF16)
    gb = jnp.where(first, high, low).astype(BF16)
    dh1 = dot_t(ga, wa[...].reshape(WP, HALF)) + dot_t(gb, wb[...].reshape(WP, HALF))
    n1, r1 = normed(xp[...].astype(F32))
    gain_part[...] = jnp.sum(dh1 * n1, axis=0, keepdims=True)
    grad = dx1[...] + norm_back(dh1 * gain[...], n1, r1)
    high_part = grad.astype(BF16)
    rest = grad - high_part.astype(F32)
    mid_part = rest.astype(BF16)
    low_part = (rest - mid_part.astype(F32)).astype(BF16)
    tokens_grad[...] = dot_t(high_part, e[...]) + (
        dot_t(mid_part, e[...]) + dot_t(low_part, e[...])
    )


def proj_grad_kernel(h_near, h_far, o_near, o_far, grads_in, order, edge, gains, out):
    h1 = jnp.concatenate([h_near[...].reshape(2 * T, WP), h_far[...].reshape(2 * T, WP)], axis=0)
    ol = jnp.concatenate([o_near[...].reshape(2 * T, WP), o_far[...].reshape(2 * T, WP)], axis=0)
    grads = jnp.concatenate([grads_in[order[k]] for k in range(4)], axis=0)
    total = jnp.where(edge[...] < QKV, tdot(h1, grads), tdot(ol, grads))
    out[...] = total.astype(BF16).reshape(NB, 32, QUART)
    out[:, 30:31, :] = gains[...]


def shards(
    tokens,
    positions,
    out_grad,
    attn_gain,
    w_query,
    key_weight,
    value_weight,
    w_out,
    mlp_gain,
    w_gate,
    w_up,
    w_down,
):
    i = lax.broadcasted_iota(jnp.int32, (WIDTH, WP), 0)
    j = lax.broadcasted_iota(jnp.int32, (WIDTH, WP), 1)
    block = i // BLK
    place = (block % 16) * 2 + block // 16
    spread = (j == place * PADB + i % BLK).astype(BF16)
    tensor = lax.axis_index("tensor")
    core = (tensor % 2).reshape(1, 1).astype(jnp.int32)

    def gain_row(gain, width):
        return jnp.pad(gain, (0, width - BLK)).reshape(1, width)

    (w1_send,) = call(
        first_kernel, [((NB, PADB, HALF), BF16)],
        w_query, key_weight, value_weight, gain_row(attn_gain, HALF), core,
    )
    w1a = exchange(w1_send, CS)
    w1b = swap(w1a, "tensor", 1)
    gain1 = w1a[:, 30, :PADB].reshape(1, WP).astype(F32)
    own_mlp, own_out = call(
        shard_kernel, [((96, FFS), BF16), ((PADB, WP), BF16)],
        w_gate, w_up, w_down, w_out, gain_row(mlp_gain, FFS), spread,
    )
    w2 = gathered(own_out)
    w3 = gathered(own_mlp)
    gain2 = w3[:, 30, :PADB].reshape(1, WP).astype(F32)

    half = D // 2
    freq = ROPE_BASE ** (-2.0 * jnp.arange(half, dtype=F32) / D)
    theta = positions.reshape(T).astype(F32)[:, None] * freq
    c, s = jnp.cos(theta), jnp.sin(theta)
    cos = jnp.concatenate([c, c, c, c], axis=1)
    sin = jnp.concatenate([-s, s, -s, s], axis=1)

    xp, dyp = call(
        pad_kernel,
        [((T, WP), BF16), ((T, WP), BF16)],
        tokens.reshape(T, WIDTH),
        out_grad.reshape(T, WIDTH),
        spread,
    )
    dy_near, dy_far = from_tensor(dyp)

    send, h1 = call(
        project_kernel,
        [((64, 80, 128), BF16), ((T, WP), BF16)],
        xp, gain1, w1a, w1b, core, cos, sin,
        scratch=[pltpu.VMEM((T, 1280), F32)],
    )
    recv = exchange(send, CT)

    lane = jnp.arange(QN, dtype=jnp.int32)
    qpos = (
        64 * ((lane % T) // 16)
        + 32 * (lax.axis_index("tensor") % 2)
        + 16 * (lane // T)
        + lane % 16
    ).reshape(1, QN)
    o_send, o_cols, lse = call(
        attend_kernel,
        [((64, 16, 128), BF16), ((QB, D, QN), F32), ((QB, 8, QN), F32)],
        recv, qpos,
        scratch=[pltpu.VMEM((QB, 128, KB), BF16), pltpu.VMEM((QB, KB, QN), F32)],
    )
    o_recv = exchange(o_send, CT)

    olp, x1, h2 = call(
        out_kernel,
        [((T, WP), BF16), ((T, WP), F32), ((T, WP), BF16)],
        o_recv, xp, spread, gain2, w2,
        scratch=[pltpu.VMEM((T, WIDTH), BF16)],
    )
    h2_near, h2_far = from_tensor(h2)
    h1_near, h1_far = from_tensor(h1)
    ol_near, ol_far = from_tensor(olp)

    tiles = [((2, T, WP), BF16)] * 4 + [((4, T, FFS), BF16)] * 3
    part, part_far, dh2, dh2_far, act, dgate, dup = call(
        mlp_kernel, tiles, h2_near, h2_far, dy_near, dy_far, w3
    )

    def summed(own, far):
        return (own.astype(F32) + swap(far, "tensor", 1).astype(F32)).astype(BF16)

    dh2 = summed(dh2, dh2_far)
    dh2_away = swap(dh2[1], "tensor", 2)
    (mlp_grad,) = call(
        mlp_grad_kernel, [((NB, 96, FFS), BF16)],
        h2_near, h2_far, dy_near, dy_far, act, dgate, dup,
    )

    dx1, da, d_send, gain2_part = call(
        mid_back_kernel,
        [((T, WP), F32), ((T, WIDTH), BF16), ((64, 16, 128), BF16), ((1, WP), F32)],
        dh2, dh2_away, x1, gain2, dyp, w2, spread,
        scratch=[pltpu.VMEM((T, WIDTH), BF16)],
    )
    d_recv = exchange(d_send, CT)
    mlp_sum = scattered(mlp_grad)
    part = summed(part, part_far)
    part_away = swap(part[1], "tensor", 2)
    (mixed,) = call(mixed_kernel, [((T, WIDTH), BF16)], part, part_away, x1, spread)

    (back_send,) = call(
        attend_back_kernel,
        [((64, 80, 128), BF16)],
        recv, qpos, d_recv, o_cols, lse,
        scratch=[pltpu.VMEM((QB, D, KB), BF16), pltpu.VMEM((QB, KB, 128), F32)],
    )
    back_recv = exchange(back_send, CT)

    full, dq_send = call(
        unpack_back_kernel,
        [((T, QKV), BF16), ((4, T, QUART), BF16)],
        back_recv, cos, sin, da,
        scratch=[pltpu.VMEM((T, 1280), F32)],
    )
    dq_recv = exchange(dq_send, "tensor")
    tokens_grad, gain1_part = call(
        tokens_back_kernel,
        [((T, WIDTH), F32), ((1, WP), F32)],
        full, w1a, w1b, core, xp, gain1, dx1, spread,
    )
    gains = jnp.concatenate(
        [gain1_part.reshape(NB, PADB), gain2_part.reshape(NB, PADB)], axis=1
    ).astype(BF16)
    gains = jnp.pad(gains, ((0, 0), (0, QUART - 2 * PADB))).reshape(NB, 1, QUART)
    order = jnp.bitwise_xor(tensor, jnp.array([0, 2, 1, 3], jnp.int32))
    edge = (tensor * QUART + jnp.arange(QUART, dtype=jnp.int32)).reshape(1, QUART)
    (proj_grad,) = call(
        proj_grad_kernel, [((NB, 32, QUART), BF16)],
        h1_near, h1_far, ol_near, ol_far, dq_recv, order, edge, gains,
        specs={5: pl.BlockSpec(memory_space=pltpu.SMEM)},
    )
    proj_sum = jnp.sum(exchange(proj_grad, CS).astype(F32), axis=0)

    near, far = from_tensor(proj_sum.astype(BF16))
    quads = jnp.concatenate([near, far], axis=0)
    gain_sums = jnp.sum(quads[:, 30, : 2 * PADB].astype(F32), axis=0)
    quarters = []
    for q in range(4):
        apart = jnp.bitwise_xor(tensor, q)
        at = (apart % 2) * 2 + apart // 2
        quarters.append(lax.dynamic_index_in_dim(quads, at, 0, keepdims=False)[:BLK])
    proj_full = jnp.concatenate(quarters, axis=1).astype(F32)
    wout_grad = proj_full[:, QKV:]
    return (
        mixed.reshape(tokens.shape),
        tokens_grad.reshape(tokens.shape),
        gain_sums[:BLK],
        proj_full[:, :960],
        proj_full[:, 960:1280],
        proj_full[:, 1280:1600],
        wout_grad,
        gain_sums[PADB : PADB + BLK],
        mlp_sum[:BLK],
        mlp_sum[32 : 32 + BLK],
        mlp_sum[64 : 64 + BLK].T,
    )


def solution(mesh):
    tok = P("shard", ("context", "tensor"), None)
    vec = P(SC)
    row = P(SC, None)
    wide = P(SC, "tensor")
    return jax.shard_map(
        shards,
        mesh=mesh,
        in_specs=(
            tok, P("shard", ("context", "tensor")), tok,
            vec, row, row, row, row, vec, wide, wide, P("tensor", SC),
        ),
        out_specs=(
            tok, tok, vec, row, row, row, row, vec, wide, wide, P("tensor", SC),
        ),
        check_vma=False,
    )
```

```python
import math

import jax
import jax.numpy as jnp
from jax import lax
from jax.experimental import pallas as pl
from jax.experimental.pallas import tpu as pltpu
from jax.sharding import PartitionSpec as P

QH = 15
KH = 5
REP = 3
D = 64
WIDTH = 960
BLK = 30
PADB = 32
NB = 32
WP = NB * PADB
QKV = 1600
FFS = 640
QUART = 640
HALF = 832
T = 128
EPSILON = 1e-05
ROPE_BASE = 100000.0
MASKED = -1e30
F32 = jnp.float32
BF16 = jnp.bfloat16
HIGHEST = lax.Precision.HIGHEST
SC = ("shard", "context")
CS = ("context", "shard")
CT = ("context", "tensor")
ALL = ("shard", "context", "tensor")
QB = 8
KB = 512
QN = 256


def dot(a, b, precision=None):
    return lax.dot_general(
        a, b, (((1,), (0,)), ((), ())), precision=precision, preferred_element_type=F32
    )


def dot_t(a, b, precision=None):
    return lax.dot_general(
        a, b, (((1,), (1,)), ((), ())), precision=precision, preferred_element_type=F32
    )


def tdot(a, b):
    return lax.dot_general(a, b, (((0,), (0,)), ((), ())), preferred_element_type=F32)


def call(fn, outs, *args, scratch=(), specs=None):
    whole = pl.BlockSpec(memory_space=pltpu.VMEM)
    return pl.pallas_call(
        fn,
        in_specs=[(specs or {}).get(k, whole) for k in range(len(args))],
        out_specs=tuple(whole for _ in outs),
        out_shape=tuple(jax.ShapeDtypeStruct(s, d) for s, d in outs),
        scratch_shapes=list(scratch),
        compiler_params=pltpu.CompilerParams(vmem_limit_bytes=56 * 1024 * 1024),
    )(*args)


def exchange(v, axes):
    return lax.all_to_all(v, axes, 0, 0, tiled=True)


def to_all(v, axes):
    n = math.prod(lax.axis_size(a) for a in ((axes,) if isinstance(axes, str) else axes))
    return exchange(jnp.broadcast_to(v, (n, *v.shape)), axes)


def swap(v, axis, bit):
    pairs = [(i, i ^ bit) for i in range(lax.axis_size(axis))]
    return lax.ppermute(v, axis, pairs)


def from_pair(v):
    return jnp.stack([v, swap(v, "tensor", 2)])


def from_tensor(v):
    near = from_pair(v)
    return near, swap(near, "tensor", 1)


def gathered(v):
    mine = lax.axis_index("shard") == 0
    other = swap(v, "shard", 1)
    pair = jnp.concatenate([jnp.where(mine, v, other), jnp.where(mine, other, v)], axis=0)
    return lax.all_gather(pair, "context", axis=0, tiled=True).reshape(NB, *v.shape)


def scattered(v):
    n = v.shape[1]
    flat = v.reshape(NB * n, v.shape[2])
    part = lax.psum_scatter(flat, "context", scatter_dimension=0, tiled=True)
    mine = lax.axis_index("shard") == 0
    keep = jnp.where(mine, part[:n], part[n:])
    away = jnp.where(mine, part[n:], part[:n])
    return keep.astype(F32) + swap(away, "shard", 1).astype(F32)


def normed(x):
    r = lax.rsqrt(jnp.sum(x * x, axis=-1, keepdims=True) * (1.0 / WIDTH) + EPSILON)
    return x * r, r


def norm_back(m, n, r):
    return r * (m - n * (jnp.sum(m * n, axis=-1, keepdims=True) * (1.0 / WIDTH)))


def turn(x, cos, sin):
    lane = lax.broadcasted_iota(jnp.int32, x.shape, 1)
    partner = jnp.where(
        lax.rem(lane, 64) < 32, pltpu.roll(x, 96, 1), pltpu.roll(x, 32, 1)
    )
    return x * cos + partner * sin


def units():
    for s in range(2):
        for head in range(QH):
            for half in range(2):
                unit = s * 30 + head * 2 + half
                yield unit, s * 64 + half * 32, head * D


def pack_rows(src, send, first):
    for unit, row, col in units():
        send[unit, first : first + 16, :] = jnp.concatenate(
            [src[row : row + 16, col : col + D], src[row + 16 : row + 32, col : col + D]], axis=1
        ).astype(send.dtype)


def unpack_rows(recv, dst, first):
    for unit, row, col in units():
        part = recv[unit, first : first + 16, :].astype(dst.dtype)
        dst[row : row + 16, col : col + D] = part[:, :D]
        dst[row + 16 : row + 32, col : col + D] = part[:, D:]


def first_kernel(wq, wk, wv, gain, core, out):
    zero = jnp.zeros((BLK, 64), BF16)
    low = wq[:, :HALF]
    high = jnp.concatenate([wq[:, HALF:], wk[...], wv[...], zero], axis=1)
    half = jnp.where(core[...] == 0, low.astype(F32), high.astype(F32)).astype(BF16)
    tail = jnp.concatenate(
        [gain[...].astype(F32), jnp.zeros((1, HALF - BLK), F32)], axis=1
    )
    tail = jnp.concatenate([tail, jnp.zeros_like(tail)], axis=0).astype(BF16)
    block = jnp.concatenate([half, tail], axis=0)
    for b in range(NB):
        out[b] = block


def shard_kernel(wg, wu, wd, wo, gain, e, out):
    i = lax.broadcasted_iota(jnp.int32, (PADB, BLK), 0)
    j = lax.broadcasted_iota(jnp.int32, (PADB, BLK), 1)
    eye = (i == j).astype(F32).astype(BF16)
    out[:, 0:FFS] = dot(eye, wg[...]).astype(BF16)
    out[:, FFS : 2 * FFS] = dot(eye, wu[...]).astype(BF16)
    out[:, 2 * FFS : 3 * FFS] = dot(eye, wd[...]).astype(BF16)
    row = lax.broadcasted_iota(jnp.int32, (PADB, WP), 0)
    tail = jnp.concatenate([gain[...].astype(F32), jnp.zeros((1, WP - BLK), F32)], axis=1)
    own = dot(eye, dot(wo[...], e[...]).astype(BF16))
    out[:, 3 * FFS :] = jnp.where(row == BLK, tail, own).astype(BF16)


def pad_kernel(x, dy, e, xp, dyp):
    xp[...] = dot(x[...], e[...]).astype(BF16)
    dyp[...] = dot(dy[...], e[...]).astype(BF16)


def project_kernel(xp, gain, wa, wb, core, cos, sin, send, h1_out, rows):
    n1, _ = normed(xp[...].astype(F32))
    h1 = (n1 * gain[...]).astype(BF16)
    h1_out[...] = h1
    ya = dot(h1, wa[...].reshape(WP, HALF))
    yb = dot(h1, wb[...].reshape(WP, HALF))
    first = core[...] == 0
    low = jnp.where(first, ya, yb)
    high = jnp.where(first, yb, ya)
    qkv = jnp.concatenate([low, high[:, : QKV - HALF]], axis=1)
    for j in range(10):
        part = turn(qkv[:, 128 * j : 128 * j + 128], cos[...], sin[...])
        rows[:, 128 * j : 128 * j + 128] = part
    send[60:64] = jnp.zeros((4, 48, 128), BF16)
    for unit, row, col in units():
        send[unit, 32:48, :] = (
            jnp.concatenate(
                [rows[row : row + 16, col : col + D], rows[row + 16 : row + 32, col : col + D]],
                axis=1,
            ).astype(BF16)
            * 0.125
        ).astype(BF16)
    for s in range(2):
        for g in range(KH):
            both = jnp.concatenate(
                [
                    rows[s * 64 : s * 64 + 64, 960 + D * g : 960 + D * g + D],
                    qkv[s * 64 : s * 64 + 64, 1280 + D * g : 1280 + D * g + D],
                ],
                axis=1,
            ).astype(BF16)
            for u in range(6):
                send[s * 30 + g * 6 + u, 0:32, :] = both[32 * (u % 2) : 32 * (u % 2) + 32]


def low_pair(block):
    lane = lax.broadcasted_iota(jnp.int32, block.shape, 1)
    zero = jnp.zeros_like(block)
    return jnp.concatenate(
        [
            jnp.where(lane < D, block, zero),
            jnp.where(lane < D, pltpu.roll(block, D, 1), zero),
        ],
        axis=0,
    ).astype(BF16)


def high_pair(block):
    lane = lax.broadcasted_iota(jnp.int32, block.shape, 1)
    zero = jnp.zeros_like(block)
    return jnp.concatenate(
        [
            jnp.where(lane >= D, pltpu.roll(block, D, 1), zero),
            jnp.where(lane >= D, block, zero),
        ],
        axis=0,
    ).astype(BF16)


def load_pair(ref, qb, first):
    return ref[qb * 8 : qb * 8 + 8, first : first + 16, :].reshape(T, 128).astype(F32)


def unpair(cols):
    flat = cols.T
    return jnp.concatenate([flat[:T], flat[T:]], axis=1).astype(BF16).reshape(8, 16, 128)


def key_block(recv, peer, kb):
    own = recv[kb * 8 : kb * 8 + 8, 0:32, :].reshape(KB // 2, 128)
    other = peer[kb * 8 : kb * 8 + 8].reshape(KB // 2, 128)
    return jnp.concatenate([own, other], axis=0)


def masked(raw, kpos, qpos):
    return jnp.where(kpos[...] <= qpos[...], raw, MASKED)


def attend_kernel(recv, peer, kpos, qpos, send, o_out, lse_out, kv_t, scores):
    for kb in range(QB):
        kv_t[kb] = key_block(recv, peer, kb).astype(F32).T.astype(BF16)
    for qb in range(QB):
        q = low_pair(load_pair(recv, qb, 32))
        top = jnp.full((8, QN), MASKED, F32)
        for kb in range(qb + 1):
            raw = dot_t(key_block(recv, peer, kb), q)
            if kb == qb:
                raw = masked(raw, kpos, qpos)
            scores[kb] = raw
            top = jnp.maximum(top, jnp.max(raw.reshape(KB // 8, 8, QN), axis=0))
        top = jnp.max(top, axis=0, keepdims=True)
        mass = jnp.zeros((8, QN), F32)
        acc = jnp.zeros((D, QN), F32)
        for kb in range(qb + 1):
            p = jnp.exp(scores[kb] - top)
            mass = mass + jnp.sum(p.reshape(KB // 8, 8, QN), axis=0)
            acc = acc + dot(kv_t[kb, D:, :], p.astype(BF16))
        mass = jnp.sum(mass, axis=0, keepdims=True)
        acc = acc / mass
        o_out[qb] = acc
        lse_out[qb] = jnp.broadcast_to(top + jnp.log(mass), (8, QN))
        send[qb * 8 : qb * 8 + 8] = unpair(acc)


def attend_back_kernel(recv, peer, kpos, qpos, core, drecv, o_in, lse_in, send, kv_t, dkv):
    for kb in range(QB):
        kv_t[kb] = key_block(recv, peer, kb)[:, :D].astype(F32).T.astype(BF16)
    dkv[...] = jnp.zeros_like(dkv)
    for qb in range(QB):
        q = low_pair(load_pair(recv, qb, 32))
        pair = load_pair(drecv, qb, 0)
        dz = high_pair(pair)
        flat = jnp.concatenate([pair[:, :D], pair[:, D:]], axis=0)
        delta = jnp.sum(flat.T * o_in[qb], axis=0, keepdims=True)
        lse = lse_in[qb][0:1]
        acc = jnp.zeros((D, QN), F32)
        for kb in range(qb + 1):
            block = key_block(recv, peer, kb)
            raw = dot_t(block, q)
            if kb == qb:
                raw = masked(raw, kpos, qpos)
            p = jnp.exp(raw - lse)
            ds = (p * (dot_t(block, dz) - delta)).astype(BF16)
            dkv[kb] += dot(ds, q) + dot(p.astype(BF16), dz)
            acc = acc + dot(kv_t[kb], ds)
        send[qb * 8 : qb * 8 + 8, 64:80, :] = unpair(acc * 0.125)
    for kb in range(QB):
        own = dkv[kb, : KB // 2, :]
        other = dkv[kb, KB // 2 :, :]
        low = jnp.where(core[...] == 0, own, other)
        high = jnp.where(core[...] == 0, other, own)
        send[kb * 8 : kb * 8 + 8, 0:32, :] = low.astype(BF16).reshape(8, 32, 128)
        send[kb * 8 : kb * 8 + 8, 32:64, :] = high.astype(BF16).reshape(8, 32, 128)


def out_kernel(recv, xp, e, gain, w, olp_out, x1_out, h2_out, ol):
    unpack_rows(recv, ol, 0)
    olp = dot(ol[...], e[...]).astype(BF16)
    olp_out[...] = olp
    x1 = xp[...].astype(F32) + dot(olp, w[:, :, 3 * FFS :].reshape(WP, WP))
    x1_out[...] = x1
    n2, _ = normed(x1)
    h2_out[...] = (n2 * gain[...]).astype(BF16)


def mlp_kernel(near, far, dnear, dfar, w, dh2, dh2_far, act, dgate, dup):
    wg = w[:, :, 0:FFS].reshape(WP, FFS)
    wu = w[:, :, FFS : 2 * FFS].reshape(WP, FFS)
    wd = w[:, :, 2 * FFS : 3 * FFS].reshape(WP, FFS)
    for i in (2, 3, 0, 1):
        h = near[i] if i < 2 else far[i - 2]
        dy = dnear[i] if i < 2 else dfar[i - 2]
        gate = dot(h, wg)
        up = dot(h, wu)
        dact = dot(dy, wd)
        sig = jax.nn.sigmoid(gate)
        silu = gate * sig
        act[i] = (silu * up).astype(BF16)
        dg = (dact * up * sig * (1.0 + gate * (1.0 - sig))).astype(BF16)
        du = (dact * silu).astype(BF16)
        dgate[i] = dg
        dup[i] = du
        back = (dot_t(dg, wg) + dot_t(du, wu)).astype(BF16)
        if i < 2:
            dh2[i] = back
        else:
            dh2_far[i - 2] = back


def mlp_part_kernel(act, w, part, part_far):
    wd = w[:, :, 2 * FFS : 3 * FFS].reshape(WP, FFS)
    for i in range(4):
        y = dot_t(act[i], wd).astype(BF16)
        if i < 2:
            part[i] = y
        else:
            part_far[i - 2] = y


def mlp_grad_kernel(near, far, dnear, dfar, act, dgate, dup, out):
    h = jnp.concatenate([near[...].reshape(2 * T, WP), far[...].reshape(2 * T, WP)], axis=0)
    d = jnp.concatenate([dnear[...].reshape(2 * T, WP), dfar[...].reshape(2 * T, WP)], axis=0)
    out[:, 0:32, :] = tdot(h, dgate[...].reshape(4 * T, FFS)).astype(BF16).reshape(NB, 32, FFS)
    out[:, 32:64, :] = tdot(h, dup[...].reshape(4 * T, FFS)).astype(BF16).reshape(NB, 32, FFS)
    out[:, 64:96, :] = tdot(d, act[...].reshape(4 * T, FFS)).astype(BF16).reshape(NB, 32, FFS)


def mixed_kernel(own, away, x1, e, out):
    total = own[0].astype(F32) + away[...].astype(F32)
    out[...] = dot_t((x1[...] + total).astype(BF16), e[...]).astype(BF16)


def mid_back_kernel(own, away, x1, gain, dyp, w, e, dx1_out, da_out, send, gain_part, dol):
    dh2 = own[0].astype(F32) + away[...].astype(F32)
    n2, r2 = normed(x1[...])
    gain_part[...] = jnp.sum(dh2 * n2, axis=0, keepdims=True)
    dx1 = dyp[...].astype(F32) + norm_back(dh2 * gain[...], n2, r2)
    dx1_out[...] = dx1
    da = dx1.astype(BF16)
    da_out[...] = dot_t(da, e[...]).astype(BF16)
    wide = dot_t(da, w[:, :, 3 * FFS :].reshape(WP, WP)).astype(BF16)
    dol[...] = dot_t(wide, e[...]).astype(BF16)
    send[60:64] = jnp.zeros((4, 16, 128), BF16)
    pack_rows(dol, send, 0)


def unpack_back_kernel(recv, cos, sin, da, full, send, rows):
    unpack_rows(recv, rows, 64)
    for s in range(2):
        for g in range(KH):
            total = recv[s * 30 + g * 6, 0:64, :].astype(F32)
            for u in range(1, 6):
                total = total + recv[s * 30 + g * 6 + u, 0:64, :].astype(F32)
            rows[s * 64 : s * 64 + 64, 960 + D * g : 960 + D * g + D] = total[:, :D]
            full[s * 64 : s * 64 + 64, 1280 + D * g : 1280 + D * g + D] = total[:, D:].astype(BF16)
    for j in range(10):
        full[:, 128 * j : 128 * j + 128] = turn(
            rows[:, 128 * j : 128 * j + 128], cos[...], -sin[...]
        ).astype(BF16)
    for t in range(4):
        first = QUART * t
        inside = min(max(QKV - first, 0), QUART)
        if inside:
            send[t, :, :inside] = full[:, first : first + inside]
        if inside < QUART:
            start = first + inside - QKV
            send[t, :, inside:] = da[:, start : start + QUART - inside]


def tokens_back_kernel(full, wa, wb, core, xp, gain, dx1, e, tokens_grad, gain_part):
    low = full[:, :HALF].astype(F32)
    high = jnp.concatenate([full[:, HALF:], jnp.zeros((T, 64), BF16)], axis=1).astype(F32)
    first = core[...] == 0
    ga = jnp.where(first, low, high).astype(BF16)
    gb = jnp.where(first, high, low).astype(BF16)
    dh1 = dot_t(ga, wa[...].reshape(WP, HALF)) + dot_t(gb, wb[...].reshape(WP, HALF))
    n1, r1 = normed(xp[...].astype(F32))
    gain_part[...] = jnp.sum(dh1 * n1, axis=0, keepdims=True)
    grad = dx1[...] + norm_back(dh1 * gain[...], n1, r1)
    high_part = grad.astype(BF16)
    rest = grad - high_part.astype(F32)
    mid_part = rest.astype(BF16)
    low_part = (rest - mid_part.astype(F32)).astype(BF16)
    tokens_grad[...] = dot_t(high_part, e[...]) + (
        dot_t(mid_part, e[...]) + dot_t(low_part, e[...])
    )


def proj_grad_kernel(h_near, h_far, o_near, o_far, grads_in, order, edge, gains, out):
    h1 = jnp.concatenate([h_near[...].reshape(2 * T, WP), h_far[...].reshape(2 * T, WP)], axis=0)
    ol = jnp.concatenate([o_near[...].reshape(2 * T, WP), o_far[...].reshape(2 * T, WP)], axis=0)
    grads = jnp.concatenate([grads_in[order[k]] for k in range(4)], axis=0)
    total = jnp.where(edge[...] < QKV, tdot(h1, grads), tdot(ol, grads))
    out[...] = total.astype(BF16).reshape(NB, 32, QUART)
    out[:, 30:31, :] = gains[...]


def shards(
    tokens,
    positions,
    out_grad,
    attn_gain,
    w_query,
    key_weight,
    value_weight,
    w_out,
    mlp_gain,
    w_gate,
    w_up,
    w_down,
):
    i = lax.broadcasted_iota(jnp.int32, (WIDTH, WP), 0)
    j = lax.broadcasted_iota(jnp.int32, (WIDTH, WP), 1)
    block = i // BLK
    place = (block % 16) * 2 + block // 16
    spread = (j == place * PADB + i % BLK).astype(BF16)
    tensor = lax.axis_index("tensor")
    core = (tensor % 2).reshape(1, 1).astype(jnp.int32)

    (w1_send,) = call(
        first_kernel, [((NB, PADB, HALF), BF16)],
        w_query, key_weight, value_weight, attn_gain.reshape(1, BLK), core,
    )
    w1a = exchange(w1_send, CS)
    gain1 = w1a[:, 30, :PADB].reshape(1, WP).astype(F32)
    w_gate, w_up, w_down, w_out, mlp_gain, tokens, w1_send = lax.optimization_barrier(
        (w_gate, w_up, w_down, w_out, mlp_gain, tokens, w1_send)
    )
    (own,) = call(
        shard_kernel, [((PADB, 3 * FFS + WP), BF16)],
        w_gate, w_up, w_down.T, w_out, mlp_gain.reshape(1, BLK), spread,
    )
    own, w1a = lax.optimization_barrier((own, w1a))
    w2 = gathered(own)
    gain2 = w2[:, 30, 3 * FFS : 3 * FFS + PADB].reshape(1, WP).astype(F32)

    half = D // 2
    freq = ROPE_BASE ** (-2.0 * jnp.arange(half, dtype=F32) / D)
    theta = positions.reshape(T).astype(F32)[:, None] * freq
    c, s = jnp.cos(theta), jnp.sin(theta)
    cos = jnp.concatenate([c, c, c, c], axis=1)
    sin = jnp.concatenate([-s, s, -s, s], axis=1)

    xp, dyp = call(
        pad_kernel,
        [((T, WP), BF16), ((T, WP), BF16)],
        tokens.reshape(T, WIDTH),
        out_grad.reshape(T, WIDTH),
        spread,
    )
    dy_near, dy_far = from_tensor(dyp)
    held, xp = lax.optimization_barrier((w1a, xp))
    w1b = swap(held, "tensor", 1)

    send, h1 = call(
        project_kernel,
        [((64, 48, 128), BF16), ((T, WP), BF16)],
        xp, gain1, w1a, w1b, core, cos, sin,
        scratch=[pltpu.VMEM((T, 1280), F32)],
    )
    recv = exchange(send, CT)
    peer = swap(recv[:, :32, :], "tensor", 1)
    h1, peer = lax.optimization_barrier((h1, peer))
    h1_near = from_pair(h1)
    row = jnp.arange(KB, dtype=jnp.int32)
    kpos = (
        64 * ((row % (KB // 2)) // 32)
        + 32 * jnp.bitwise_xor(tensor % 2, row // (KB // 2))
        + row % 32
    ).reshape(KB, 1)

    lane = jnp.arange(QN, dtype=jnp.int32)
    qpos = (
        64 * ((lane % T) // 16)
        + 32 * (lax.axis_index("tensor") % 2)
        + 16 * (lane // T)
        + lane % 16
    ).reshape(1, QN)
    o_send, o_cols, lse = call(
        attend_kernel,
        [((64, 16, 128), BF16), ((QB, D, QN), F32), ((QB, 8, QN), F32)],
        recv, peer, kpos, qpos,
        scratch=[pltpu.VMEM((QB, 128, KB), BF16), pltpu.VMEM((QB, KB, QN), F32)],
    )
    o_send, h1_near = lax.optimization_barrier((o_send, h1_near))
    h1_far = swap(h1_near, "tensor", 1)
    o_recv = exchange(o_send, CT)

    olp, x1, h2 = call(
        out_kernel,
        [((T, WP), BF16), ((T, WP), F32), ((T, WP), BF16)],
        o_recv, xp, spread, gain2, w2,
        scratch=[pltpu.VMEM((T, WIDTH), BF16)],
    )
    h2_near, h2_far = from_tensor(h2)
    olp, h2_far = lax.optimization_barrier((olp, h2_far))
    ol_near = from_pair(olp)

    tiles = [((2, T, WP), BF16)] * 2 + [((4, T, FFS), BF16)] * 3
    dh2, dh2_far, act, dgate, dup = call(
        mlp_kernel, tiles, h2_near, h2_far, dy_near, dy_far, w2
    )
    part, part_far = call(mlp_part_kernel, [((2, T, WP), BF16)] * 2, act, w2)

    def summed(own, far):
        return (own.astype(F32) + swap(far, "tensor", 1).astype(F32)).astype(BF16)

    dh2 = summed(dh2, dh2_far)
    dh2, ol_near = lax.optimization_barrier((dh2, ol_near))
    dh2_away = swap(dh2[1], "tensor", 2)
    ol_far = swap(ol_near, "tensor", 1)

    dx1, da, d_send, gain2_part = call(
        mid_back_kernel,
        [((T, WP), F32), ((T, WIDTH), BF16), ((64, 16, 128), BF16), ((1, WP), F32)],
        dh2, dh2_away, x1, gain2, dyp, w2, spread,
        scratch=[pltpu.VMEM((T, WIDTH), BF16)],
    )
    act, dgate, dup, d_send = lax.optimization_barrier((act, dgate, dup, d_send))
    d_recv = exchange(d_send, CT)
    (mlp_grad,) = call(
        mlp_grad_kernel, [((NB, 96, FFS), BF16)],
        h2_near, h2_far, dy_near, dy_far, act, dgate, dup,
    )
    mlp_sum = scattered(mlp_grad)
    part = summed(part, part_far)
    part, d_recv = lax.optimization_barrier((part, d_recv))
    part_away = swap(part[1], "tensor", 2)
    (back_send,) = call(
        attend_back_kernel,
        [((64, 80, 128), BF16)],
        recv, peer, kpos, qpos, core, d_recv, o_cols, lse,
        scratch=[pltpu.VMEM((QB, D, KB), BF16), pltpu.VMEM((QB, KB, 128), F32)],
    )
    back_send, part_away = lax.optimization_barrier((back_send, part_away))
    back_recv = exchange(back_send, CT)
    (mixed,) = call(mixed_kernel, [((T, WIDTH), BF16)], part, part_away, x1, spread)
    back_recv, mixed = lax.optimization_barrier((back_recv, mixed))

    full, dq_send = call(
        unpack_back_kernel,
        [((T, QKV), BF16), ((4, T, QUART), BF16)],
        back_recv, cos, sin, da,
        scratch=[pltpu.VMEM((T, 1280), F32)],
    )
    dq_recv = exchange(dq_send, "tensor")
    tokens_grad, gain1_part = call(
        tokens_back_kernel,
        [((T, WIDTH), F32), ((1, WP), F32)],
        full, w1a, w1b, core, xp, gain1, dx1, spread,
    )
    gains = jnp.concatenate(
        [gain1_part.reshape(NB, PADB), gain2_part.reshape(NB, PADB)], axis=1
    ).astype(BF16)
    gains = jnp.pad(gains, ((0, 0), (0, QUART - 2 * PADB))).reshape(NB, 1, QUART)
    order = jnp.bitwise_xor(tensor, jnp.array([0, 2, 1, 3], jnp.int32))
    edge = (tensor * QUART + jnp.arange(QUART, dtype=jnp.int32)).reshape(1, QUART)
    (proj_grad,) = call(
        proj_grad_kernel, [((NB, 32, QUART), BF16)],
        h1_near, h1_far, ol_near, ol_far, dq_recv, order, edge, gains,
        specs={5: pl.BlockSpec(memory_space=pltpu.SMEM)},
    )
    proj_sum = jnp.sum(exchange(proj_grad, CS).astype(F32), axis=0)

    near, far = from_tensor(proj_sum.astype(BF16))
    quads = jnp.concatenate([near, far], axis=0)
    gain_sums = jnp.sum(quads[:, 30, : 2 * PADB].astype(F32), axis=0)
    quarters = []
    for q in range(4):
        apart = jnp.bitwise_xor(tensor, q)
        at = (apart % 2) * 2 + apart // 2
        quarters.append(lax.dynamic_index_in_dim(quads, at, 0, keepdims=False)[:BLK])
    proj_full = jnp.concatenate(quarters, axis=1).astype(F32)
    wout_grad = proj_full[:, QKV:]
    return (
        mixed.reshape(tokens.shape),
        tokens_grad.reshape(tokens.shape),
        gain_sums[:BLK],
        proj_full[:, :960],
        proj_full[:, 960:1280],
        proj_full[:, 1280:1600],
        wout_grad,
        gain_sums[PADB : PADB + BLK],
        mlp_sum[:BLK],
        mlp_sum[32 : 32 + BLK],
        mlp_sum[64 : 64 + BLK].T,
    )


def solution(mesh):
    tok = P("shard", ("context", "tensor"), None)
    vec = P(SC)
    row = P(SC, None)
    wide = P(SC, "tensor")
    return jax.shard_map(
        shards,
        mesh=mesh,
        in_specs=(
            tok, P("shard", ("context", "tensor")), tok,
            vec, row, row, row, row, vec, wide, wide, P("tensor", SC),
        ),
        out_specs=(
            tok, tok, vec, row, row, row, row, vec, wide, wide, P("tensor", SC),
        ),
        check_vma=False,
    )
```

```python
import math

import jax
import jax.numpy as jnp
import numpy as np
from jax import lax
from jax.experimental import pallas as pl
from jax.experimental.pallas import tpu as pltpu
from jax.sharding import PartitionSpec as P

QH = 15
KH = 5
REP = 3
D = 64
WIDTH = 960
BLK = 30
PADB = 32
NB = 32
WP = NB * PADB
QKV = 1600
FFS = 640
QUART = 640
HALF = 832
T = 128
EPSILON = 1e-05
ROPE_BASE = 100000.0
MASKED = -1e30
F32 = jnp.float32
BF16 = jnp.bfloat16
HIGHEST = lax.Precision.HIGHEST
SC = ("shard", "context")
CS = ("context", "shard")
CT = ("context", "tensor")
ALL = ("shard", "context", "tensor")
QB = 8
KB = 512
QN = 256


def dot(a, b, precision=None):
    return lax.dot_general(
        a, b, (((1,), (0,)), ((), ())), precision=precision, preferred_element_type=F32
    )


def dot_t(a, b, precision=None):
    return lax.dot_general(
        a, b, (((1,), (1,)), ((), ())), precision=precision, preferred_element_type=F32
    )


def tdot(a, b):
    return lax.dot_general(a, b, (((0,), (0,)), ((), ())), preferred_element_type=F32)


def call(fn, outs, *args, scratch=(), specs=None):
    whole = pl.BlockSpec(memory_space=pltpu.VMEM)
    return pl.pallas_call(
        fn,
        in_specs=[(specs or {}).get(k, whole) for k in range(len(args))],
        out_specs=tuple(whole for _ in outs),
        out_shape=tuple(jax.ShapeDtypeStruct(s, d) for s, d in outs),
        scratch_shapes=list(scratch),
        compiler_params=pltpu.CompilerParams(vmem_limit_bytes=56 * 1024 * 1024),
    )(*args)


def exchange(v, axes):
    return lax.all_to_all(v, axes, 0, 0, tiled=True)


def to_all(v, axes):
    n = math.prod(lax.axis_size(a) for a in ((axes,) if isinstance(axes, str) else axes))
    return exchange(jnp.broadcast_to(v, (n, *v.shape)), axes)


def swap(v, axis, bit):
    pairs = [(i, i ^ bit) for i in range(lax.axis_size(axis))]
    return lax.ppermute(v, axis, pairs)


def from_pair(v):
    return jnp.stack([v, swap(v, "tensor", 2)])


def from_tensor(v):
    near = from_pair(v)
    return near, swap(near, "tensor", 1)


def paired(v):
    mine = lax.axis_index("shard") == 0
    other = swap(v, "shard", 1)
    return jnp.concatenate([jnp.where(mine, v, other), jnp.where(mine, other, v)], axis=0)


def from_each(pieces):
    return [pieces[0]] + [swap(pieces[k], "tensor", k) for k in range(1, 4)]


def scattered(v):
    n = v.shape[1]
    flat = v.reshape(NB * n, v.shape[2])
    return lax.psum_scatter(flat, "context", scatter_dimension=0, tiled=True)


def over_shard(part):
    n = part.shape[0] // 2
    mine = lax.axis_index("shard") == 0
    keep = jnp.where(mine, part[:n], part[n:])
    away = jnp.where(mine, part[n:], part[:n])
    return keep.astype(F32) + swap(away, "shard", 1).astype(F32)


def normed(x):
    r = lax.rsqrt(jnp.sum(x * x, axis=-1, keepdims=True) * (1.0 / WIDTH) + EPSILON)
    return x * r, r


def norm_back(m, n, r):
    return r * (m - n * (jnp.sum(m * n, axis=-1, keepdims=True) * (1.0 / WIDTH)))


def turn(x, cos, sin):
    lane = lax.broadcasted_iota(jnp.int32, x.shape, 1)
    partner = jnp.where(
        lax.rem(lane, 64) < 32, pltpu.roll(x, 96, 1), pltpu.roll(x, 32, 1)
    )
    return x * cos + partner * sin


def units():
    for s in range(2):
        for head in range(QH):
            for half in range(2):
                unit = s * 30 + head * 2 + half
                yield unit, s * 64 + half * 32, head * D


def pack_rows(src, send, first):
    for unit, row, col in units():
        send[unit, first : first + 16, :] = jnp.concatenate(
            [src[row : row + 16, col : col + D], src[row + 16 : row + 32, col : col + D]], axis=1
        ).astype(send.dtype)


def unpack_rows(recv, dst, first):
    for unit, row, col in units():
        part = recv[unit, first : first + 16, :].astype(dst.dtype)
        dst[row : row + 16, col : col + D] = part[:, :D]
        dst[row + 16 : row + 32, col : col + D] = part[:, D:]


def first_kernel(wq, wk, wv, gain, core, out):
    zero = jnp.zeros((BLK, 64), BF16)
    low = wq[:, :HALF]
    high = jnp.concatenate([wq[:, HALF:], wk[...], wv[...], zero], axis=1)
    half = jnp.where(core[...] == 0, low.astype(F32), high.astype(F32)).astype(BF16)
    tail = jnp.concatenate(
        [gain[...].astype(F32), jnp.zeros((1, HALF - BLK), F32)], axis=1
    )
    tail = jnp.concatenate([tail, jnp.zeros_like(tail)], axis=0).astype(BF16)
    block = jnp.concatenate([half, tail], axis=0)
    for b in range(NB):
        out[b] = block


def prep_kernel(wg, wu, wd, wo, gain, x, dy, e, out, xd):
    i = lax.broadcasted_iota(jnp.int32, (PADB, BLK), 0)
    j = lax.broadcasted_iota(jnp.int32, (PADB, BLK), 1)
    eye = (i == j).astype(F32).astype(BF16)
    out[:, 0:FFS] = dot(eye, wg[...]).astype(BF16)
    out[:, FFS : 2 * FFS] = dot(eye, wu[...]).astype(BF16)
    out[:, 2 * FFS : 3 * FFS] = dot(eye, wd[...]).astype(BF16)
    row = lax.broadcasted_iota(jnp.int32, (PADB, WP), 0)
    tail = jnp.concatenate([gain[...].astype(F32), jnp.zeros((1, WP - BLK), F32)], axis=1)
    own = dot(eye, dot(wo[...], e[...]).astype(BF16))
    out[:, 3 * FFS :] = jnp.where(row == BLK, tail, own).astype(BF16)
    xd[0] = dot(x[...], e[...]).astype(BF16)
    xd[1] = dot(dy[...], e[...]).astype(BF16)


def project_kernel(xd, gain, wa, wb, core, cos, sin, send, rows):
    n1, _ = normed(xd[0].astype(F32))
    h1 = (n1 * gain[...]).astype(BF16)
    ya = dot(h1, wa[...].reshape(WP, HALF))
    yb = dot(h1, wb[...].reshape(WP, HALF))
    first = core[...] == 0
    low = jnp.where(first, ya, yb)
    high = jnp.where(first, yb, ya)
    qkv = jnp.concatenate([low, high[:, : QKV - HALF]], axis=1)
    for j in range(10):
        part = turn(qkv[:, 128 * j : 128 * j + 128], cos[...], sin[...])
        rows[:, 128 * j : 128 * j + 128] = part
    send[60:64] = jnp.zeros((4, 48, 128), BF16)
    for unit, row, col in units():
        send[unit, 32:48, :] = (
            jnp.concatenate(
                [rows[row : row + 16, col : col + D], rows[row + 16 : row + 32, col : col + D]],
                axis=1,
            ).astype(BF16)
            * 0.125
        ).astype(BF16)
    for s in range(2):
        for g in range(KH):
            both = jnp.concatenate(
                [
                    rows[s * 64 : s * 64 + 64, 960 + D * g : 960 + D * g + D],
                    qkv[s * 64 : s * 64 + 64, 1280 + D * g : 1280 + D * g + D],
                ],
                axis=1,
            ).astype(BF16)
            for u in range(6):
                send[s * 30 + g * 6 + u, 0:32, :] = both[32 * (u % 2) : 32 * (u % 2) + 32]


def hidden_kernel(x0, x1, x2, x3, gain, out):
    for k, x in enumerate((x0, x1, x2, x3)):
        n1, _ = normed(x[0].astype(F32))
        out[T * k : T * k + T, :] = (n1 * gain[...]).astype(BF16)


def low_pair(block):
    lane = lax.broadcasted_iota(jnp.int32, block.shape, 1)
    zero = jnp.zeros_like(block)
    return jnp.concatenate(
        [
            jnp.where(lane < D, block, zero),
            jnp.where(lane < D, pltpu.roll(block, D, 1), zero),
        ],
        axis=0,
    ).astype(BF16)


def high_pair(block):
    lane = lax.broadcasted_iota(jnp.int32, block.shape, 1)
    zero = jnp.zeros_like(block)
    return jnp.concatenate(
        [
            jnp.where(lane >= D, pltpu.roll(block, D, 1), zero),
            jnp.where(lane >= D, block, zero),
        ],
        axis=0,
    ).astype(BF16)


def load_pair(ref, qb, first):
    return ref[qb * 8 : qb * 8 + 8, first : first + 16, :].reshape(T, 128).astype(F32)


def unpair(cols):
    flat = cols.T
    return jnp.concatenate([flat[:T], flat[T:]], axis=1).astype(BF16).reshape(8, 16, 128)


def key_block(recv, peer, kb):
    own = recv[kb * 8 : kb * 8 + 8, 0:32, :].reshape(KB // 2, 128)
    other = peer[kb * 8 : kb * 8 + 8].reshape(KB // 2, 128)
    return jnp.concatenate([own, other], axis=0)


def masked(raw, kpos, qpos):
    return jnp.where(kpos[...] <= qpos[...], raw, MASKED)


def attend_kernel(recv, peer, kpos, qpos, send, o_out, lse_out, kv_t, scores):
    for kb in range(QB):
        kv_t[kb] = key_block(recv, peer, kb).astype(F32).T.astype(BF16)
    for qb in range(QB):
        q = low_pair(load_pair(recv, qb, 32))
        top = jnp.full((8, QN), MASKED, F32)
        for kb in range(qb + 1):
            raw = dot_t(key_block(recv, peer, kb), q)
            if kb == qb:
                raw = masked(raw, kpos, qpos)
            scores[kb] = raw
            top = jnp.maximum(top, jnp.max(raw.reshape(KB // 8, 8, QN), axis=0))
        top = jnp.max(top, axis=0, keepdims=True)
        mass = jnp.zeros((8, QN), F32)
        acc = jnp.zeros((D, QN), F32)
        for kb in range(qb + 1):
            p = jnp.exp(scores[kb] - top)
            mass = mass + jnp.sum(p.reshape(KB // 8, 8, QN), axis=0)
            acc = acc + dot(kv_t[kb, D:, :], p.astype(BF16))
        mass = jnp.sum(mass, axis=0, keepdims=True)
        acc = acc / mass
        o_out[qb] = acc
        lse_out[qb] = jnp.broadcast_to(top + jnp.log(mass), (8, QN))
        send[qb * 8 : qb * 8 + 8] = unpair(acc)


def attend_back_kernel(recv, peer, kpos, qpos, core, drecv, o_in, lse_in, send, kv_t, dkv):
    for kb in range(QB):
        kv_t[kb] = key_block(recv, peer, kb)[:, :D].astype(F32).T.astype(BF16)
    dkv[...] = jnp.zeros_like(dkv)
    for qb in range(QB):
        q = low_pair(load_pair(recv, qb, 32))
        pair = load_pair(drecv, qb, 0)
        dz = high_pair(pair)
        flat = jnp.concatenate([pair[:, :D], pair[:, D:]], axis=0)
        delta = jnp.sum(flat.T * o_in[qb], axis=0, keepdims=True)
        lse = lse_in[qb][0:1]
        acc = jnp.zeros((D, QN), F32)
        for kb in range(qb + 1):
            block = key_block(recv, peer, kb)
            raw = dot_t(block, q)
            if kb == qb:
                raw = masked(raw, kpos, qpos)
            p = jnp.exp(raw - lse)
            ds = (p * (dot_t(block, dz) - delta)).astype(BF16)
            dkv[kb] += dot(ds, q) + dot(p.astype(BF16), dz)
            acc = acc + dot(kv_t[kb], ds)
        send[qb * 8 : qb * 8 + 8, 64:80, :] = unpair(acc * 0.125)
    for kb in range(QB):
        own = dkv[kb, : KB // 2, :]
        other = dkv[kb, KB // 2 :, :]
        low = jnp.where(core[...] == 0, own, other)
        high = jnp.where(core[...] == 0, other, own)
        send[kb * 8 : kb * 8 + 8, 0:32, :] = low.astype(BF16).reshape(8, 32, 128)
        send[kb * 8 : kb * 8 + 8, 32:64, :] = high.astype(BF16).reshape(8, 32, 128)


def out_kernel(recv, xd, e, gain, w, olp_out, x1_out, h2_out, ol):
    unpack_rows(recv, ol, 0)
    olp = dot(ol[...], e[...]).astype(BF16)
    olp_out[...] = olp
    x1 = xd[0].astype(F32) + dot(olp, w[:, :, 3 * FFS :].reshape(WP, WP))
    x1_out[...] = x1
    n2, _ = normed(x1)
    h2_out[...] = (n2 * gain[...]).astype(BF16)


def mlp_kernel(h_a, h_b, dy_a, dy_b, w, back_a, back_b, act, dgate, dup):
    wg = w[:, :, 0:FFS].reshape(WP, FFS)
    wu = w[:, :, FFS : 2 * FFS].reshape(WP, FFS)
    wd = w[:, :, 2 * FFS : 3 * FFS].reshape(WP, FFS)
    for i, (h_in, dy_in, back) in enumerate(((h_a, dy_a, back_a), (h_b, dy_b, back_b))):
        h = h_in[...]
        gate = dot(h, wg)
        up = dot(h, wu)
        dact = dot(dy_in[1], wd)
        sig = jax.nn.sigmoid(gate)
        silu = gate * sig
        act[i] = (silu * up).astype(BF16)
        dg = (dact * up * sig * (1.0 + gate * (1.0 - sig))).astype(BF16)
        du = (dact * silu).astype(BF16)
        dgate[i] = dg
        dup[i] = du
        back[...] = (dot_t(dg, wg) + dot_t(du, wu)).astype(BF16)


def mlp_part_kernel(near, far, w, part, part_far):
    wd = w[:, :, 2 * FFS : 3 * FFS].reshape(WP, FFS)
    part[0] = dot_t(near[0], wd).astype(BF16)
    part[1] = dot_t(far[0], wd).astype(BF16)
    part_far[0] = dot_t(near[1], wd).astype(BF16)
    part_far[1] = dot_t(far[1], wd).astype(BF16)


def mlp_grad_kernel(
    h0, h1, h2, h3, d0, d1, d2, d3, act_n, act_f, gate_n, gate_f, up_n, up_f, out
):
    h = jnp.concatenate([h0[...], h1[...], h2[...], h3[...]], axis=0)
    d = jnp.concatenate([d0[1], d1[1], d2[1], d3[1]], axis=0)
    for k, (left, near, far) in enumerate(((h, gate_n, gate_f), (h, up_n, up_f), (d, act_n, act_f))):
        right = jnp.concatenate(
            [near[...].reshape(2 * T, FFS), far[...].reshape(2 * T, FFS)], axis=0
        )
        out[:, 32 * k : 32 * k + 32, :] = tdot(left, right).astype(BF16).reshape(NB, 32, FFS)


def mixed_kernel(own, away, x1, e, out):
    total = own[0].astype(F32) + away[...].astype(F32)
    out[...] = dot_t((x1[...] + total).astype(BF16), e[...]).astype(BF16)


def mid_back_kernel(
    b0, b1, b2, b3, x1, gain, xd, w, e, dx1_out, da_out, send, gain_part, dol
):
    dh2 = (b0[...].astype(F32) + b1[...].astype(F32)) + (
        b2[...].astype(F32) + b3[...].astype(F32)
    )
    n2, r2 = normed(x1[...])
    gain_part[...] = jnp.sum(dh2 * n2, axis=0, keepdims=True)
    dx1 = xd[1].astype(F32) + norm_back(dh2 * gain[...], n2, r2)
    dx1_out[...] = dx1
    da = dx1.astype(BF16)
    da_out[...] = dot_t(da, e[...]).astype(BF16)
    wide = dot_t(da, w[:, :, 3 * FFS :].reshape(WP, WP)).astype(BF16)
    dol[...] = dot_t(wide, e[...]).astype(BF16)
    send[60:64] = jnp.zeros((4, 16, 128), BF16)
    pack_rows(dol, send, 0)


def unpack_back_kernel(recv, cos, sin, da, slot, full, s0, s1, s2, s3, rows, held):
    unpack_rows(recv, rows, 64)
    for s in range(2):
        for g in range(KH):
            total = recv[s * 30 + g * 6, 0:64, :].astype(F32)
            for u in range(1, 6):
                total = total + recv[s * 30 + g * 6 + u, 0:64, :].astype(F32)
            rows[s * 64 : s * 64 + 64, 960 + D * g : 960 + D * g + D] = total[:, :D]
            full[s * 64 : s * 64 + 64, 1280 + D * g : 1280 + D * g + D] = total[:, D:].astype(BF16)
    for j in range(10):
        full[:, 128 * j : 128 * j + 128] = turn(
            rows[:, 128 * j : 128 * j + 128], cos[...], -sin[...]
        ).astype(BF16)
    for t in range(4):
        first = QUART * t
        inside = min(max(QKV - first, 0), QUART)
        if inside:
            held[t, :, :inside] = full[:, first : first + inside]
        if inside < QUART:
            start = first + inside - QKV
            held[t, :, inside:] = da[:, start : start + QUART - inside]
    for k, out in enumerate((s0, s1, s2, s3)):
        out[...] = held[slot[k]]


def tokens_back_kernel(full, wa, wb, core, xd, gain, dx1, e, tokens_grad, gain_part):
    low = full[:, :HALF].astype(F32)
    high = jnp.concatenate([full[:, HALF:], jnp.zeros((T, 64), BF16)], axis=1).astype(F32)
    first = core[...] == 0
    ga = jnp.where(first, low, high).astype(BF16)
    gb = jnp.where(first, high, low).astype(BF16)
    dh1 = dot_t(ga, wa[...].reshape(WP, HALF)) + dot_t(gb, wb[...].reshape(WP, HALF))
    n1, r1 = normed(xd[0].astype(F32))
    gain_part[...] = jnp.sum(dh1 * n1, axis=0, keepdims=True)
    grad = dx1[...] + norm_back(dh1 * gain[...], n1, r1)
    high_part = grad.astype(BF16)
    rest = grad - high_part.astype(F32)
    mid_part = rest.astype(BF16)
    low_part = (rest - mid_part.astype(F32)).astype(BF16)
    tokens_grad[...] = dot_t(high_part, e[...]) + (
        dot_t(mid_part, e[...]) + dot_t(low_part, e[...])
    )


def proj_grad_kernel(h1_all, o_near, o_far, g0, g1, g2, g3, edge, gains, out):
    ol = jnp.concatenate([o_near[0], o_far[0], o_near[1], o_far[1]], axis=0)
    grads = jnp.concatenate([g0[...], g1[...], g2[...], g3[...]], axis=0)
    total = jnp.where(edge[...] < QKV, tdot(h1_all[...], grads), tdot(ol, grads))
    out[...] = total.astype(BF16).reshape(NB, 32, QUART)
    out[:, 30:31, :] = gains[...]


def total_kernel(pieces, out):
    total = pieces[0].astype(F32)
    for b in range(1, NB):
        total = total + pieces[b].astype(F32)
    out[...] = total.astype(BF16)


def last_kernel(p0, p1, p2, p3, slot, wq, wk, wv, wo, gains, held):
    for k, p in enumerate((p0, p1, p2, p3)):
        held[k] = p[...].astype(F32)
    gains[...] = held[0, 30:31, :] + held[1, 30:31, :] + held[2, 30:31, :] + held[3, 30:31, :]
    full = jnp.concatenate([held[slot[q], :BLK, :] for q in range(4)], axis=1)
    wq[...] = full[:, :960]
    wk[...] = full[:, 960:1280]
    wv[...] = full[:, 1280:QKV]
    wo[...] = full[:, QKV:]


def shards(
    tokens,
    positions,
    out_grad,
    attn_gain,
    w_query,
    key_weight,
    value_weight,
    w_out,
    mlp_gain,
    w_gate,
    w_up,
    w_down,
):
    at = np.arange(WIDTH)
    block = at // BLK
    table = np.zeros((WIDTH, WP), np.float32)
    table[at, ((block % 16) * 2 + block // 16) * PADB + at % BLK] = 1.0
    spread = jnp.asarray(table, BF16)
    tensor = lax.axis_index("tensor")
    core = (tensor % 2).reshape(1, 1).astype(jnp.int32)

    (w1_send,) = call(
        first_kernel, [((NB, PADB, HALF), BF16)],
        w_query, key_weight, value_weight, attn_gain.reshape(1, BLK), core,
    )
    w1a = exchange(w1_send, CS)
    w_gate, w_up, w_down, w_out, mlp_gain, w1_send = lax.optimization_barrier(
        (w_gate, w_up, w_down, w_out, mlp_gain, w1_send)
    )
    own, xd = call(
        prep_kernel,
        [((PADB, 3 * FFS + WP), BF16), ((2, T, WP), BF16)],
        w_gate, w_up, w_down.T, w_out, mlp_gain.reshape(1, BLK),
        tokens.reshape(T, WIDTH), out_grad.reshape(T, WIDTH), spread,
    )
    half = D // 2
    freq = ROPE_BASE ** (-2.0 * jnp.arange(half, dtype=F32) / D)
    theta = positions.reshape(T).astype(F32)[:, None] * freq
    c, s = jnp.cos(theta), jnp.sin(theta)
    cos = jnp.concatenate([c, c, c, c], axis=1)
    sin = jnp.concatenate([-s, s, -s, s], axis=1)

    w1a, own, xd, cos, sin = lax.optimization_barrier((w1a, own, xd, cos, sin))
    w1b = swap(w1a, "tensor", 1)
    w2 = lax.all_gather(paired(own), "context", axis=0, tiled=True).reshape(NB, *own.shape)
    gain2 = w2[:, 30, 3 * FFS : 3 * FFS + PADB].reshape(1, WP).astype(F32)
    gain1 = w1a[:, 30, :PADB].reshape(1, WP).astype(F32)

    (send,) = call(
        project_kernel,
        [((64, 48, 128), BF16)],
        xd, gain1, w1a, w1b, core, cos, sin,
        scratch=[pltpu.VMEM((T, 1280), F32)],
    )
    recv = exchange(send, CT)
    peer = swap(recv[:, :32, :], "tensor", 1)
    row = jnp.arange(KB, dtype=jnp.int32)
    kpos = (
        64 * ((row % (KB // 2)) // 32)
        + 32 * jnp.bitwise_xor(tensor % 2, row // (KB // 2))
        + row % 32
    ).reshape(KB, 1)

    lane = jnp.arange(QN, dtype=jnp.int32)
    qpos = (
        64 * ((lane % T) // 16)
        + 32 * (lax.axis_index("tensor") % 2)
        + 16 * (lane // T)
        + lane % 16
    ).reshape(1, QN)
    o_send, o_cols, lse = call(
        attend_kernel,
        [((64, 16, 128), BF16), ((QB, D, QN), F32), ((QB, 8, QN), F32)],
        recv, peer, kpos, qpos,
        scratch=[pltpu.VMEM((QB, 128, KB), BF16), pltpu.VMEM((QB, KB, QN), F32)],
    )
    o_recv = exchange(o_send, CT)
    xd, o_send = lax.optimization_barrier((xd, o_send))
    xd_one, xd_two = swap(xd, "tensor", 1), swap(xd, "tensor", 2)

    olp, x1, h2 = call(
        out_kernel,
        [((T, WP), BF16), ((T, WP), F32), ((T, WP), BF16)],
        o_recv, xd, spread, gain2, w2,
        scratch=[pltpu.VMEM((T, WIDTH), BF16)],
    )
    h2, xd_two = lax.optimization_barrier((h2, xd_two))
    xd_three = swap(xd_two, "tensor", 1)
    h2_one, h2_two, h2_three = (swap(h2, "tensor", k) for k in (1, 2, 3))
    tiles = [((T, WP), BF16)] * 2 + [((2, T, FFS), BF16)] * 3
    back0, back1, act_n, gate_n, up_n = call(
        mlp_kernel, tiles, h2, h2_one, xd, xd_one, w2
    )
    h2_two, h2_three, back1 = lax.optimization_barrier((h2_two, h2_three, back1))
    back2, back3, act_f, gate_f, up_f = call(
        mlp_kernel, tiles, h2_two, h2_three, xd_two, xd_three, w2
    )
    back1, back2, back3 = (swap(b, "tensor", k + 1) for k, b in enumerate((back1, back2, back3)))
    (mlp_grad,) = call(
        mlp_grad_kernel, [((NB, 96, FFS), BF16)],
        h2, h2_one, h2_two, h2_three, xd, xd_one, xd_two, xd_three,
        act_n, act_f, gate_n, gate_f, up_n, up_f,
    )
    part, part_far = call(mlp_part_kernel, [((2, T, WP), BF16)] * 2, act_n, act_f, w2)
    back1, back2, back3, mlp_grad, part, part_far = lax.optimization_barrier(
        (back1, back2, back3, mlp_grad, part, part_far)
    )
    mlp_part = scattered(mlp_grad)

    dx1, da, d_send, gain2_part = call(
        mid_back_kernel,
        [((T, WP), F32), ((T, WIDTH), BF16), ((64, 16, 128), BF16), ((1, WP), F32)],
        back0, back1, back2, back3, x1, gain2, xd, w2, spread,
        scratch=[pltpu.VMEM((T, WIDTH), BF16)],
    )
    d_recv = exchange(d_send, CT)
    part_far, olp, d_send = lax.optimization_barrier((part_far, olp, d_send))
    part = part.astype(F32) + swap(part_far, "tensor", 1).astype(F32)
    part = part.astype(BF16)
    d_recv, part = lax.optimization_barrier((d_recv, part))
    part_away = swap(part[1], "tensor", 2)
    ol_near = from_pair(olp)
    (back_send,) = call(
        attend_back_kernel,
        [((64, 80, 128), BF16)],
        recv, peer, kpos, qpos, core, d_recv, o_cols, lse,
        scratch=[pltpu.VMEM((QB, D, KB), BF16), pltpu.VMEM((QB, KB, 128), F32)],
    )
    back_send, part_away, ol_near = lax.optimization_barrier((back_send, part_away, ol_near))
    ol_far = swap(ol_near, "tensor", 1)
    back_recv = exchange(back_send, CT)
    (mixed,) = call(mixed_kernel, [((T, WIDTH), BF16)], part, part_away, x1, spread)
    (h1_all,) = call(
        hidden_kernel, [((4 * T, WP), BF16)], xd, xd_one, xd_two, xd_three, gain1
    )
    back_recv, mixed, h1_all = lax.optimization_barrier((back_recv, mixed, h1_all))

    slot = jnp.bitwise_xor(tensor, jnp.arange(4, dtype=jnp.int32))
    full, *dq_send = call(
        unpack_back_kernel,
        [((T, QKV), BF16)] + [((T, QUART), BF16)] * 4,
        back_recv, cos, sin, da, slot,
        specs={4: pl.BlockSpec(memory_space=pltpu.SMEM)},
        scratch=[pltpu.VMEM((T, 1280), F32), pltpu.VMEM((4, T, QUART), BF16)],
    )
    dq_recv = from_each(dq_send)
    tokens_grad, gain1_part = call(
        tokens_back_kernel,
        [((T, WIDTH), F32), ((1, WP), F32)],
        full, w1a, w1b, core, xd, gain1, dx1, spread,
    )
    gains = jnp.concatenate(
        [gain1_part.reshape(NB, PADB), gain2_part.reshape(NB, PADB)], axis=1
    ).astype(BF16)
    gains = jnp.pad(gains, ((0, 0), (0, QUART - 2 * PADB))).reshape(NB, 1, QUART)
    edge = (tensor * QUART + jnp.arange(QUART, dtype=jnp.int32)).reshape(1, QUART)
    (proj_grad,) = call(
        proj_grad_kernel, [((NB, 32, QUART), BF16)],
        h1_all, ol_near, ol_far, *dq_recv, edge, gains,
    )
    proj_recv = exchange(proj_grad, CS)
    mlp_part, proj_grad = lax.optimization_barrier((mlp_part, proj_grad))
    mlp_sum = over_shard(mlp_part)
    (proj_sum,) = call(total_kernel, [((32, QUART), BF16)], proj_recv)
    wq_grad, wk_grad, wv_grad, wo_grad, gain_sums = call(
        last_kernel,
        [((BLK, 960), F32), ((BLK, 320), F32), ((BLK, 320), F32), ((BLK, 960), F32), ((1, QUART), F32)],
        *from_each([proj_sum] * 4), slot,
        specs={4: pl.BlockSpec(memory_space=pltpu.SMEM)},
        scratch=[pltpu.VMEM((4, 32, QUART), F32)],
    )
    gain_sums = gain_sums[0]
    return (
        mixed.reshape(tokens.shape),
        tokens_grad.reshape(tokens.shape),
        gain_sums[:BLK],
        wq_grad,
        wk_grad,
        wv_grad,
        wo_grad,
        gain_sums[PADB : PADB + BLK],
        mlp_sum[:BLK],
        mlp_sum[32 : 32 + BLK],
        mlp_sum[64 : 64 + BLK].T,
    )


def solution(mesh):
    tok = P("shard", ("context", "tensor"), None)
    vec = P(SC)
    row = P(SC, None)
    wide = P(SC, "tensor")
    return jax.shard_map(
        shards,
        mesh=mesh,
        in_specs=(
            tok, P("shard", ("context", "tensor")), tok,
            vec, row, row, row, row, vec, wide, wide, P("tensor", SC),
        ),
        out_specs=(
            tok, tok, vec, row, row, row, row, vec, wide, wide, P("tensor", SC),
        ),
        check_vma=False,
    )
```

```python
import math

import jax
import jax.numpy as jnp
import numpy as np
from jax import lax
from jax.experimental import pallas as pl
from jax.experimental.pallas import tpu as pltpu
from jax.sharding import PartitionSpec as P

QH = 15
KH = 5
REP = 3
D = 64
WIDTH = 960
BLK = 30
PADB = 32
NB = 32
WP = NB * PADB
QKV = 1600
FFS = 640
QUART = 640
HALF = 832
T = 128
EPSILON = 1e-05
ROPE_BASE = 100000.0
MASKED = -1e30
F32 = jnp.float32
BF16 = jnp.bfloat16
HIGHEST = lax.Precision.HIGHEST
SC = ("shard", "context")
CS = ("context", "shard")
CT = ("context", "tensor")
ALL = ("shard", "context", "tensor")
QB = 8
KB = 512
QN = 256


def dot(a, b, precision=None):
    return lax.dot_general(
        a, b, (((1,), (0,)), ((), ())), precision=precision, preferred_element_type=F32
    )


def dot_t(a, b, precision=None):
    return lax.dot_general(
        a, b, (((1,), (1,)), ((), ())), precision=precision, preferred_element_type=F32
    )


def tdot(a, b):
    return lax.dot_general(a, b, (((0,), (0,)), ((), ())), preferred_element_type=F32)


def call(fn, outs, *args, scratch=(), specs=None):
    whole = pl.BlockSpec(memory_space=pltpu.VMEM)
    return pl.pallas_call(
        fn,
        in_specs=[(specs or {}).get(k, whole) for k in range(len(args))],
        out_specs=tuple(whole for _ in outs),
        out_shape=tuple(jax.ShapeDtypeStruct(s, d) for s, d in outs),
        scratch_shapes=list(scratch),
        compiler_params=pltpu.CompilerParams(vmem_limit_bytes=56 * 1024 * 1024),
    )(*args)


def exchange(v, axes):
    return lax.all_to_all(v, axes, 0, 0, tiled=True)


def to_all(v, axes):
    n = math.prod(lax.axis_size(a) for a in ((axes,) if isinstance(axes, str) else axes))
    return exchange(jnp.broadcast_to(v, (n, *v.shape)), axes)


def swap(v, axis, bit):
    pairs = [(i, i ^ bit) for i in range(lax.axis_size(axis))]
    return lax.ppermute(v, axis, pairs)


def from_pair(v):
    return jnp.stack([v, swap(v, "tensor", 2)])


def from_tensor(v):
    near = from_pair(v)
    return near, swap(near, "tensor", 1)


def from_each(pieces):
    return [pieces[0]] + [swap(pieces[k], "tensor", k) for k in range(1, 4)]


def scattered(v):
    n = v.shape[1]
    flat = v.reshape(NB * n, v.shape[2])
    return lax.psum_scatter(flat, "context", scatter_dimension=0, tiled=True)


def over_shard(part):
    n = part.shape[0] // 2
    mine = lax.axis_index("shard") == 0
    keep = jnp.where(mine, part[:n], part[n:])
    away = jnp.where(mine, part[n:], part[:n])
    return keep.astype(F32) + swap(away, "shard", 1).astype(F32)


def normed(x):
    r = lax.rsqrt(jnp.sum(x * x, axis=-1, keepdims=True) * (1.0 / WIDTH) + EPSILON)
    return x * r, r


def norm_back(m, n, r):
    return r * (m - n * (jnp.sum(m * n, axis=-1, keepdims=True) * (1.0 / WIDTH)))


def turn(x, cos, sin):
    lane = lax.broadcasted_iota(jnp.int32, x.shape, 1)
    partner = jnp.where(
        lax.rem(lane, 64) < 32, pltpu.roll(x, 96, 1), pltpu.roll(x, 32, 1)
    )
    return x * cos + partner * sin


def units():
    for s in range(2):
        for head in range(QH):
            for half in range(2):
                unit = s * 30 + head * 2 + half
                yield unit, s * 64 + half * 32, head * D


def pack_rows(src, send, first):
    for unit, row, col in units():
        send[unit, first : first + 16, :] = jnp.concatenate(
            [src[row : row + 16, col : col + D], src[row + 16 : row + 32, col : col + D]], axis=1
        ).astype(send.dtype)


def unpack_rows(recv, dst, first):
    for unit, row, col in units():
        part = recv[unit, first : first + 16, :].astype(dst.dtype)
        dst[row : row + 16, col : col + D] = part[:, :D]
        dst[row + 16 : row + 32, col : col + D] = part[:, D:]


def first_kernel(wq, wk, wv, gain, core, out):
    zero = jnp.zeros((BLK, 64), BF16)
    low = wq[:, :HALF]
    high = jnp.concatenate([wq[:, HALF:], wk[...], wv[...], zero], axis=1)
    half = jnp.where(core[...] == 0, low.astype(F32), high.astype(F32)).astype(BF16)
    tail = jnp.concatenate(
        [gain[...].astype(F32), jnp.zeros((1, HALF - BLK), F32)], axis=1
    )
    tail = jnp.concatenate([tail, jnp.zeros_like(tail)], axis=0).astype(BF16)
    block = jnp.concatenate([half, tail], axis=0)
    for b in range(NB):
        out[b] = block


def prep_kernel(own, other, shard, x, dy, e, out, xd):
    i = lax.broadcasted_iota(jnp.int32, (PADB, BLK), 0)
    j = lax.broadcasted_iota(jnp.int32, (PADB, BLK), 1)
    eye = (i == j).astype(F32).astype(BF16)
    row = lax.broadcasted_iota(jnp.int32, (PADB, WP), 0)
    mine = shard[...] == 0
    rows = 3 * FFS

    def block(v):
        tail = jnp.concatenate(
            [v[BLK : BLK + 1, :BLK].astype(F32), jnp.zeros((1, WP - BLK), F32)], axis=1
        )
        wide = dot(v[:BLK, rows:], e[...]).astype(BF16)
        return dot(eye, v[:BLK, :rows]), jnp.where(row == BLK, tail, dot(eye, wide))

    mlp_own, out_own = block(own)
    mlp_other, out_other = block(other)
    out[0:PADB, :rows] = jnp.where(mine, mlp_own, mlp_other).astype(BF16)
    out[PADB:, :rows] = jnp.where(mine, mlp_other, mlp_own).astype(BF16)
    out[0:PADB, rows:] = jnp.where(mine, out_own, out_other).astype(BF16)
    out[PADB:, rows:] = jnp.where(mine, out_other, out_own).astype(BF16)
    xd[0] = dot(x[...], e[...]).astype(BF16)
    xd[1] = dot(dy[...], e[...]).astype(BF16)


def project_kernel(xd, gain, wa, wb, core, cos, sin, send, rows):
    n1, _ = normed(xd[0].astype(F32))
    h1 = (n1 * gain[...]).astype(BF16)
    ya = dot(h1, wa[...].reshape(WP, HALF))
    yb = dot(h1, wb[...].reshape(WP, HALF))
    first = core[...] == 0
    low = jnp.where(first, ya, yb)
    high = jnp.where(first, yb, ya)
    qkv = jnp.concatenate([low, high[:, : QKV - HALF]], axis=1)
    for j in range(10):
        part = turn(qkv[:, 128 * j : 128 * j + 128], cos[...], sin[...])
        rows[:, 128 * j : 128 * j + 128] = part
    send[60:64] = jnp.zeros((4, 48, 128), BF16)
    for unit, row, col in units():
        send[unit, 32:48, :] = (
            jnp.concatenate(
                [rows[row : row + 16, col : col + D], rows[row + 16 : row + 32, col : col + D]],
                axis=1,
            ).astype(BF16)
            * 0.125
        ).astype(BF16)
    for s in range(2):
        for g in range(KH):
            both = jnp.concatenate(
                [
                    rows[s * 64 : s * 64 + 64, 960 + D * g : 960 + D * g + D],
                    qkv[s * 64 : s * 64 + 64, 1280 + D * g : 1280 + D * g + D],
                ],
                axis=1,
            ).astype(BF16)
            for u in range(6):
                send[s * 30 + g * 6 + u, 0:32, :] = both[32 * (u % 2) : 32 * (u % 2) + 32]


def hidden_kernel(x0, x1, x2, x3, gain, out):
    for k, x in enumerate((x0, x1, x2, x3)):
        n1, _ = normed(x[0].astype(F32))
        out[T * k : T * k + T, :] = (n1 * gain[...]).astype(BF16)


def low_pair(block):
    lane = lax.broadcasted_iota(jnp.int32, block.shape, 1)
    zero = jnp.zeros_like(block)
    return jnp.concatenate(
        [
            jnp.where(lane < D, block, zero),
            jnp.where(lane < D, pltpu.roll(block, D, 1), zero),
        ],
        axis=0,
    ).astype(BF16)


def high_pair(block):
    lane = lax.broadcasted_iota(jnp.int32, block.shape, 1)
    zero = jnp.zeros_like(block)
    return jnp.concatenate(
        [
            jnp.where(lane >= D, pltpu.roll(block, D, 1), zero),
            jnp.where(lane >= D, block, zero),
        ],
        axis=0,
    ).astype(BF16)


def load_pair(ref, qb, first):
    return ref[qb * 8 : qb * 8 + 8, first : first + 16, :].reshape(T, 128).astype(F32)


def unpair(cols):
    flat = cols.T
    return jnp.concatenate([flat[:T], flat[T:]], axis=1).astype(BF16).reshape(8, 16, 128)


def key_block(recv, peer, kb):
    own = recv[kb * 8 : kb * 8 + 8, 0:32, :].reshape(KB // 2, 128)
    other = peer[kb * 8 : kb * 8 + 8].reshape(KB // 2, 128)
    return jnp.concatenate([own, other], axis=0)


def masked(raw, kpos, qpos):
    return jnp.where(kpos[...] <= qpos[...], raw, MASKED)


def attend_kernel(recv, peer, kpos, qpos, send, o_out, lse_out, kv_t, scores):
    for kb in range(QB):
        kv_t[kb] = key_block(recv, peer, kb).astype(F32).T.astype(BF16)
    for qb in range(QB):
        q = low_pair(load_pair(recv, qb, 32))
        top = jnp.full((8, QN), MASKED, F32)
        for kb in range(qb + 1):
            raw = dot_t(key_block(recv, peer, kb), q)
            if kb == qb:
                raw = masked(raw, kpos, qpos)
            scores[kb] = raw
            top = jnp.maximum(top, jnp.max(raw.reshape(KB // 8, 8, QN), axis=0))
        top = jnp.max(top, axis=0, keepdims=True)
        mass = jnp.zeros((8, QN), F32)
        acc = jnp.zeros((D, QN), F32)
        for kb in range(qb + 1):
            p = jnp.exp(scores[kb] - top)
            mass = mass + jnp.sum(p.reshape(KB // 8, 8, QN), axis=0)
            acc = acc + dot(kv_t[kb, D:, :], p.astype(BF16))
        mass = jnp.sum(mass, axis=0, keepdims=True)
        acc = acc / mass
        o_out[qb] = acc
        lse_out[qb] = jnp.broadcast_to(top + jnp.log(mass), (8, QN))
        send[qb * 8 : qb * 8 + 8] = unpair(acc)


def attend_back_kernel(recv, peer, kpos, qpos, core, drecv, o_in, lse_in, send, kv_t, dkv):
    for kb in range(QB):
        kv_t[kb] = key_block(recv, peer, kb)[:, :D].astype(F32).T.astype(BF16)
    dkv[...] = jnp.zeros_like(dkv)
    for qb in range(QB):
        q = low_pair(load_pair(recv, qb, 32))
        pair = load_pair(drecv, qb, 0)
        dz = high_pair(pair)
        flat = jnp.concatenate([pair[:, :D], pair[:, D:]], axis=0)
        delta = jnp.sum(flat.T * o_in[qb], axis=0, keepdims=True)
        lse = lse_in[qb][0:1]
        acc = jnp.zeros((D, QN), F32)
        for kb in range(qb + 1):
            block = key_block(recv, peer, kb)
            raw = dot_t(block, q)
            if kb == qb:
                raw = masked(raw, kpos, qpos)
            p = jnp.exp(raw - lse)
            ds = (p * (dot_t(block, dz) - delta)).astype(BF16)
            dkv[kb] += dot(ds, q) + dot(p.astype(BF16), dz)
            acc = acc + dot(kv_t[kb], ds)
        send[qb * 8 : qb * 8 + 8, 64:80, :] = unpair(acc * 0.125)
    for kb in range(QB):
        own = dkv[kb, : KB // 2, :]
        other = dkv[kb, KB // 2 :, :]
        low = jnp.where(core[...] == 0, own, other)
        high = jnp.where(core[...] == 0, other, own)
        send[kb * 8 : kb * 8 + 8, 0:32, :] = low.astype(BF16).reshape(8, 32, 128)
        send[kb * 8 : kb * 8 + 8, 32:64, :] = high.astype(BF16).reshape(8, 32, 128)


def out_kernel(recv, xd, e, gain, w, olp_out, x1_out, h2_out, ol):
    unpack_rows(recv, ol, 0)
    olp = dot(ol[...], e[...]).astype(BF16)
    olp_out[...] = olp
    x1 = xd[0].astype(F32) + dot(olp, w[:, :, 3 * FFS :].reshape(WP, WP))
    x1_out[...] = x1
    n2, _ = normed(x1)
    h2_out[...] = (n2 * gain[...]).astype(BF16)


def mlp_kernel(h_a, h_b, dy_a, dy_b, w, back_a, back_b, act, dgate, dup):
    wg = w[:, :, 0:FFS].reshape(WP, FFS)
    wu = w[:, :, FFS : 2 * FFS].reshape(WP, FFS)
    wd = w[:, :, 2 * FFS : 3 * FFS].reshape(WP, FFS)
    for i, (h_in, dy_in, back) in enumerate(((h_a, dy_a, back_a), (h_b, dy_b, back_b))):
        h = h_in[...]
        gate = dot(h, wg)
        up = dot(h, wu)
        dact = dot(dy_in[1], wd)
        sig = jax.nn.sigmoid(gate)
        silu = gate * sig
        act[i] = (silu * up).astype(BF16)
        dg = (dact * up * sig * (1.0 + gate * (1.0 - sig))).astype(BF16)
        du = (dact * silu).astype(BF16)
        dgate[i] = dg
        dup[i] = du
        back[...] = (dot_t(dg, wg) + dot_t(du, wu)).astype(BF16)


def mlp_part_kernel(near, far, w, part, part_far):
    wd = w[:, :, 2 * FFS : 3 * FFS].reshape(WP, FFS)
    part[0] = dot_t(near[0], wd).astype(BF16)
    part[1] = dot_t(far[0], wd).astype(BF16)
    part_far[0] = dot_t(near[1], wd).astype(BF16)
    part_far[1] = dot_t(far[1], wd).astype(BF16)


def mlp_grad_kernel(
    h0, h1, h2, h3, d0, d1, d2, d3, act_n, act_f, gate_n, gate_f, up_n, up_f, out
):
    h = jnp.concatenate([h0[...], h1[...], h2[...], h3[...]], axis=0)
    d = jnp.concatenate([d0[1], d1[1], d2[1], d3[1]], axis=0)
    for k, (left, near, far) in enumerate(((h, gate_n, gate_f), (h, up_n, up_f), (d, act_n, act_f))):
        right = jnp.concatenate(
            [near[...].reshape(2 * T, FFS), far[...].reshape(2 * T, FFS)], axis=0
        )
        out[:, 32 * k : 32 * k + 32, :] = tdot(left, right).astype(BF16).reshape(NB, 32, FFS)


def mixed_kernel(own, away, x1, e, out):
    total = own[0].astype(F32) + away[...].astype(F32)
    out[...] = dot_t((x1[...] + total).astype(BF16), e[...]).astype(BF16)


def mid_back_kernel(
    b0, b1, b2, b3, x1, gain, xd, w, e, dx1_out, da_out, send, gain_part, dol
):
    dh2 = (b0[...].astype(F32) + b1[...].astype(F32)) + (
        b2[...].astype(F32) + b3[...].astype(F32)
    )
    n2, r2 = normed(x1[...])
    gain_part[...] = jnp.sum(dh2 * n2, axis=0, keepdims=True)
    dx1 = xd[1].astype(F32) + norm_back(dh2 * gain[...], n2, r2)
    dx1_out[...] = dx1
    da = dx1.astype(BF16)
    da_out[...] = dot_t(da, e[...]).astype(BF16)
    wide = dot_t(da, w[:, :, 3 * FFS :].reshape(WP, WP)).astype(BF16)
    dol[...] = dot_t(wide, e[...]).astype(BF16)
    send[60:64] = jnp.zeros((4, 16, 128), BF16)
    pack_rows(dol, send, 0)


def unpack_back_kernel(recv, cos, sin, da, slot, full, s0, s1, s2, s3, rows, held):
    unpack_rows(recv, rows, 64)
    for s in range(2):
        for g in range(KH):
            total = recv[s * 30 + g * 6, 0:64, :].astype(F32)
            for u in range(1, 6):
                total = total + recv[s * 30 + g * 6 + u, 0:64, :].astype(F32)
            rows[s * 64 : s * 64 + 64, 960 + D * g : 960 + D * g + D] = total[:, :D]
            full[s * 64 : s * 64 + 64, 1280 + D * g : 1280 + D * g + D] = total[:, D:].astype(BF16)
    for j in range(10):
        full[:, 128 * j : 128 * j + 128] = turn(
            rows[:, 128 * j : 128 * j + 128], cos[...], -sin[...]
        ).astype(BF16)
    for t in range(4):
        first = QUART * t
        inside = min(max(QKV - first, 0), QUART)
        if inside:
            held[t, :, :inside] = full[:, first : first + inside]
        if inside < QUART:
            start = first + inside - QKV
            held[t, :, inside:] = da[:, start : start + QUART - inside]
    for k, out in enumerate((s0, s1, s2, s3)):
        out[...] = held[slot[k]]


def tokens_back_kernel(full, wa, wb, core, xd, gain, dx1, e, tokens_grad, gain_part):
    low = full[:, :HALF].astype(F32)
    high = jnp.concatenate([full[:, HALF:], jnp.zeros((T, 64), BF16)], axis=1).astype(F32)
    first = core[...] == 0
    ga = jnp.where(first, low, high).astype(BF16)
    gb = jnp.where(first, high, low).astype(BF16)
    dh1 = dot_t(ga, wa[...].reshape(WP, HALF)) + dot_t(gb, wb[...].reshape(WP, HALF))
    n1, r1 = normed(xd[0].astype(F32))
    gain_part[...] = jnp.sum(dh1 * n1, axis=0, keepdims=True)
    grad = dx1[...] + norm_back(dh1 * gain[...], n1, r1)
    high_part = grad.astype(BF16)
    rest = grad - high_part.astype(F32)
    mid_part = rest.astype(BF16)
    low_part = (rest - mid_part.astype(F32)).astype(BF16)
    tokens_grad[...] = dot_t(high_part, e[...]) + (
        dot_t(mid_part, e[...]) + dot_t(low_part, e[...])
    )


def proj_grad_kernel(h1_all, o_near, o_far, g0, g1, g2, g3, edge, gains, out):
    ol = jnp.concatenate([o_near[0], o_far[0], o_near[1], o_far[1]], axis=0)
    grads = jnp.concatenate([g0[...], g1[...], g2[...], g3[...]], axis=0)
    total = jnp.where(edge[...] < QKV, tdot(h1_all[...], grads), tdot(ol, grads))
    out[...] = total.astype(BF16).reshape(NB, 32, QUART)
    out[:, 30:31, :] = gains[...]


def total_kernel(pieces, out):
    total = pieces[0].astype(F32)
    for b in range(1, NB):
        total = total + pieces[b].astype(F32)
    out[...] = total.astype(BF16)


def last_kernel(p0, p1, p2, p3, slot, wq, wk, wv, wo, gains, held):
    for k, p in enumerate((p0, p1, p2, p3)):
        held[k] = p[...].astype(F32)
    gains[...] = held[0, 30:31, :] + held[1, 30:31, :] + held[2, 30:31, :] + held[3, 30:31, :]
    full = jnp.concatenate([held[slot[q], :BLK, :] for q in range(4)], axis=1)
    wq[...] = full[:, :960]
    wk[...] = full[:, 960:1280]
    wv[...] = full[:, 1280:QKV]
    wo[...] = full[:, QKV:]


def shards(
    tokens,
    positions,
    out_grad,
    attn_gain,
    w_query,
    key_weight,
    value_weight,
    w_out,
    mlp_gain,
    w_gate,
    w_up,
    w_down,
):
    at = np.arange(WIDTH)
    block = at // BLK
    table = np.zeros((WIDTH, WP), np.float32)
    table[at, ((block % 16) * 2 + block // 16) * PADB + at % BLK] = 1.0
    spread = jnp.asarray(table, BF16)
    tensor = lax.axis_index("tensor")
    core = (tensor % 2).reshape(1, 1).astype(jnp.int32)

    (w1_send,) = call(
        first_kernel, [((NB, PADB, HALF), BF16)],
        w_query, key_weight, value_weight, attn_gain.reshape(1, BLK), core,
    )
    rows = jnp.concatenate([w_gate, w_up, w_down.T, w_out], axis=1)
    gain_row = jnp.pad(mlp_gain[None, :], ((0, 0), (0, rows.shape[1] - BLK)))
    rows = jnp.concatenate([rows, gain_row], axis=0)
    other = swap(rows, "shard", 1)
    rows, other, w1_send = lax.optimization_barrier((rows, other, w1_send))
    w1a = exchange(w1_send, CS)
    shard = lax.axis_index("shard").reshape(1, 1).astype(jnp.int32)
    pair, xd = call(
        prep_kernel,
        [((2 * PADB, 3 * FFS + WP), BF16), ((2, T, WP), BF16)],
        rows, other, shard, tokens.reshape(T, WIDTH), out_grad.reshape(T, WIDTH), spread,
    )

    half = D // 2
    freq = ROPE_BASE ** (-2.0 * jnp.arange(half, dtype=F32) / D)
    theta = positions.reshape(T).astype(F32)[:, None] * freq
    c, s = jnp.cos(theta), jnp.sin(theta)
    cos = jnp.concatenate([c, c, c, c], axis=1)
    sin = jnp.concatenate([-s, s, -s, s], axis=1)

    w1a, pair, xd, cos, sin = lax.optimization_barrier((w1a, pair, xd, cos, sin))
    w1b = swap(w1a, "tensor", 1)
    w2 = lax.all_gather(pair, "context", axis=0, tiled=True).reshape(NB, PADB, -1)
    gain2 = w2[:, 30, 3 * FFS : 3 * FFS + PADB].reshape(1, WP).astype(F32)
    gain1 = w1a[:, 30, :PADB].reshape(1, WP).astype(F32)

    (send,) = call(
        project_kernel,
        [((64, 48, 128), BF16)],
        xd, gain1, w1a, w1b, core, cos, sin,
        scratch=[pltpu.VMEM((T, 1280), F32)],
    )
    recv = exchange(send, CT)
    peer = swap(recv[:, :32, :], "tensor", 1)
    row = jnp.arange(KB, dtype=jnp.int32)
    kpos = (
        64 * ((row % (KB // 2)) // 32)
        + 32 * jnp.bitwise_xor(tensor % 2, row // (KB // 2))
        + row % 32
    ).reshape(KB, 1)

    lane = jnp.arange(QN, dtype=jnp.int32)
    qpos = (
        64 * ((lane % T) // 16)
        + 32 * (lax.axis_index("tensor") % 2)
        + 16 * (lane // T)
        + lane % 16
    ).reshape(1, QN)
    o_send, o_cols, lse = call(
        attend_kernel,
        [((64, 16, 128), BF16), ((QB, D, QN), F32), ((QB, 8, QN), F32)],
        recv, peer, kpos, qpos,
        scratch=[pltpu.VMEM((QB, 128, KB), BF16), pltpu.VMEM((QB, KB, QN), F32)],
    )
    o_recv = exchange(o_send, CT)
    xd, o_send = lax.optimization_barrier((xd, o_send))
    xd_one, xd_two = swap(xd, "tensor", 1), swap(xd, "tensor", 2)

    olp, x1, h2 = call(
        out_kernel,
        [((T, WP), BF16), ((T, WP), F32), ((T, WP), BF16)],
        o_recv, xd, spread, gain2, w2,
        scratch=[pltpu.VMEM((T, WIDTH), BF16)],
    )
    h2, xd_two = lax.optimization_barrier((h2, xd_two))
    xd_three = swap(xd_two, "tensor", 1)
    h2_one, h2_two, h2_three = (swap(h2, "tensor", k) for k in (1, 2, 3))
    tiles = [((T, WP), BF16)] * 2 + [((2, T, FFS), BF16)] * 3
    back0, back1, act_n, gate_n, up_n = call(
        mlp_kernel, tiles, h2, h2_one, xd, xd_one, w2
    )
    h2_two, h2_three, back1 = lax.optimization_barrier((h2_two, h2_three, back1))
    back2, back3, act_f, gate_f, up_f = call(
        mlp_kernel, tiles, h2_two, h2_three, xd_two, xd_three, w2
    )
    back1, back2, back3 = (swap(b, "tensor", k + 1) for k, b in enumerate((back1, back2, back3)))
    (mlp_grad,) = call(
        mlp_grad_kernel, [((NB, 96, FFS), BF16)],
        h2, h2_one, h2_two, h2_three, xd, xd_one, xd_two, xd_three,
        act_n, act_f, gate_n, gate_f, up_n, up_f,
    )
    part, part_far = call(mlp_part_kernel, [((2, T, WP), BF16)] * 2, act_n, act_f, w2)
    back1, back2, back3, mlp_grad, part, part_far = lax.optimization_barrier(
        (back1, back2, back3, mlp_grad, part, part_far)
    )
    mlp_part = scattered(mlp_grad)

    dx1, da, d_send, gain2_part = call(
        mid_back_kernel,
        [((T, WP), F32), ((T, WIDTH), BF16), ((64, 16, 128), BF16), ((1, WP), F32)],
        back0, back1, back2, back3, x1, gain2, xd, w2, spread,
        scratch=[pltpu.VMEM((T, WIDTH), BF16)],
    )
    d_recv = exchange(d_send, CT)
    part_far, olp, d_send = lax.optimization_barrier((part_far, olp, d_send))
    part = part.astype(F32) + swap(part_far, "tensor", 1).astype(F32)
    part = part.astype(BF16)
    d_recv, part = lax.optimization_barrier((d_recv, part))
    part_away = swap(part[1], "tensor", 2)
    ol_near = from_pair(olp)
    (back_send,) = call(
        attend_back_kernel,
        [((64, 80, 128), BF16)],
        recv, peer, kpos, qpos, core, d_recv, o_cols, lse,
        scratch=[pltpu.VMEM((QB, D, KB), BF16), pltpu.VMEM((QB, KB, 128), F32)],
    )
    back_send, part_away, ol_near = lax.optimization_barrier((back_send, part_away, ol_near))
    ol_far = swap(ol_near, "tensor", 1)
    back_recv = exchange(back_send, CT)
    (mixed,) = call(mixed_kernel, [((T, WIDTH), BF16)], part, part_away, x1, spread)
    (h1_all,) = call(
        hidden_kernel, [((4 * T, WP), BF16)], xd, xd_one, xd_two, xd_three, gain1
    )
    back_recv, mixed, h1_all = lax.optimization_barrier((back_recv, mixed, h1_all))

    slot = jnp.bitwise_xor(tensor, jnp.arange(4, dtype=jnp.int32))
    full, *dq_send = call(
        unpack_back_kernel,
        [((T, QKV), BF16)] + [((T, QUART), BF16)] * 4,
        back_recv, cos, sin, da, slot,
        specs={4: pl.BlockSpec(memory_space=pltpu.SMEM)},
        scratch=[pltpu.VMEM((T, 1280), F32), pltpu.VMEM((4, T, QUART), BF16)],
    )
    dq_recv = from_each(dq_send)
    tokens_grad, gain1_part = call(
        tokens_back_kernel,
        [((T, WIDTH), F32), ((1, WP), F32)],
        full, w1a, w1b, core, xd, gain1, dx1, spread,
    )
    gains = jnp.concatenate(
        [gain1_part.reshape(NB, PADB), gain2_part.reshape(NB, PADB)], axis=1
    ).astype(BF16)
    gains = jnp.pad(gains, ((0, 0), (0, QUART - 2 * PADB))).reshape(NB, 1, QUART)
    edge = (tensor * QUART + jnp.arange(QUART, dtype=jnp.int32)).reshape(1, QUART)
    (proj_grad,) = call(
        proj_grad_kernel, [((NB, 32, QUART), BF16)],
        h1_all, ol_near, ol_far, *dq_recv, edge, gains,
    )
    proj_recv = exchange(proj_grad, CS)
    mlp_part, proj_grad = lax.optimization_barrier((mlp_part, proj_grad))
    mlp_sum = over_shard(mlp_part)
    proj_recv, mlp_sum = lax.optimization_barrier((proj_recv, mlp_sum))
    (proj_sum,) = call(total_kernel, [((32, QUART), BF16)], proj_recv)
    wq_grad, wk_grad, wv_grad, wo_grad, gain_sums = call(
        last_kernel,
        [((BLK, 960), F32), ((BLK, 320), F32), ((BLK, 320), F32), ((BLK, 960), F32), ((1, QUART), F32)],
        *from_each([proj_sum] * 4), slot,
        specs={4: pl.BlockSpec(memory_space=pltpu.SMEM)},
        scratch=[pltpu.VMEM((4, 32, QUART), F32)],
    )
    gain_sums = gain_sums[0]
    return (
        mixed.reshape(tokens.shape),
        tokens_grad.reshape(tokens.shape),
        gain_sums[:BLK],
        wq_grad,
        wk_grad,
        wv_grad,
        wo_grad,
        gain_sums[PADB : PADB + BLK],
        mlp_sum[:BLK],
        mlp_sum[32 : 32 + BLK],
        mlp_sum[64 : 64 + BLK].T,
    )


def solution(mesh):
    tok = P("shard", ("context", "tensor"), None)
    vec = P(SC)
    row = P(SC, None)
    wide = P(SC, "tensor")
    return jax.shard_map(
        shards,
        mesh=mesh,
        in_specs=(
            tok, P("shard", ("context", "tensor")), tok,
            vec, row, row, row, row, vec, wide, wide, P("tensor", SC),
        ),
        out_specs=(
            tok, tok, vec, row, row, row, row, vec, wide, wide, P("tensor", SC),
        ),
        check_vma=False,
    )
```

```python
import math

import jax
import jax.numpy as jnp
import numpy as np
from jax import lax
from jax.experimental import pallas as pl
from jax.experimental.pallas import tpu as pltpu
from jax.sharding import PartitionSpec as P

QH = 15
KH = 5
REP = 3
D = 64
WIDTH = 960
BLK = 30
PADB = 32
NB = 32
WP = NB * PADB
QKV = 1600
FFS = 640
QUART = 640
HALF = 832
T = 128
EPSILON = 1e-05
ROPE_BASE = 100000.0
MASKED = -1e30
F32 = jnp.float32
BF16 = jnp.bfloat16
HIGHEST = lax.Precision.HIGHEST
SC = ("shard", "context")
CS = ("context", "shard")
CT = ("context", "tensor")
ALL = ("shard", "context", "tensor")
QB = 8
KB = 512
QN = 256


def dot(a, b, precision=None):
    return lax.dot_general(
        a, b, (((1,), (0,)), ((), ())), precision=precision, preferred_element_type=F32
    )


def dot_t(a, b, precision=None):
    return lax.dot_general(
        a, b, (((1,), (1,)), ((), ())), precision=precision, preferred_element_type=F32
    )


def tdot(a, b):
    return lax.dot_general(a, b, (((0,), (0,)), ((), ())), preferred_element_type=F32)


def call(fn, outs, *args, scratch=(), specs=None):
    whole = pl.BlockSpec(memory_space=pltpu.VMEM)
    return pl.pallas_call(
        fn,
        in_specs=[(specs or {}).get(k, whole) for k in range(len(args))],
        out_specs=tuple(whole for _ in outs),
        out_shape=tuple(jax.ShapeDtypeStruct(s, d) for s, d in outs),
        scratch_shapes=list(scratch),
        compiler_params=pltpu.CompilerParams(vmem_limit_bytes=56 * 1024 * 1024),
    )(*args)


def exchange(v, axes):
    return lax.all_to_all(v, axes, 0, 0, tiled=True)


def to_all(v, axes):
    n = math.prod(lax.axis_size(a) for a in ((axes,) if isinstance(axes, str) else axes))
    return exchange(jnp.broadcast_to(v, (n, *v.shape)), axes)


def swap(v, axis, bit):
    pairs = [(i, i ^ bit) for i in range(lax.axis_size(axis))]
    return lax.ppermute(v, axis, pairs)


def from_pair(v):
    return jnp.stack([v, swap(v, "tensor", 2)])


def from_tensor(v):
    near = from_pair(v)
    return near, swap(near, "tensor", 1)


def from_each(pieces):
    return [pieces[0]] + [swap(pieces[k], "tensor", k) for k in range(1, 4)]


def scattered(v):
    n = v.shape[1]
    flat = v.reshape(NB * n, v.shape[2])
    return lax.psum_scatter(flat, "context", scatter_dimension=0, tiled=True)


def over_shard(part):
    n = part.shape[0] // 2
    mine = lax.axis_index("shard") == 0
    keep = jnp.where(mine, part[:n], part[n:])
    away = jnp.where(mine, part[n:], part[:n])
    return keep.astype(F32) + swap(away, "shard", 1).astype(F32)


def normed(x):
    r = lax.rsqrt(jnp.sum(x * x, axis=-1, keepdims=True) * (1.0 / WIDTH) + EPSILON)
    return x * r, r


def norm_back(m, n, r):
    return r * (m - n * (jnp.sum(m * n, axis=-1, keepdims=True) * (1.0 / WIDTH)))


def turn(x, cos, sin):
    lane = lax.broadcasted_iota(jnp.int32, x.shape, 1)
    partner = jnp.where(
        lax.rem(lane, 64) < 32, pltpu.roll(x, 96, 1), pltpu.roll(x, 32, 1)
    )
    return x * cos + partner * sin


def units():
    for s in range(2):
        for head in range(QH):
            for half in range(2):
                unit = s * 30 + head * 2 + half
                yield unit, s * 64 + half * 32, head * D


def pack_rows(src, send, first):
    for unit, row, col in units():
        send[unit, first : first + 16, :] = jnp.concatenate(
            [src[row : row + 16, col : col + D], src[row + 16 : row + 32, col : col + D]], axis=1
        ).astype(send.dtype)


def unpack_rows(recv, dst, first):
    for unit, row, col in units():
        part = recv[unit, first : first + 16, :].astype(dst.dtype)
        dst[row : row + 16, col : col + D] = part[:, :D]
        dst[row + 16 : row + 32, col : col + D] = part[:, D:]


def first_kernel(wq, wk, wv, gain, core, out):
    zero = jnp.zeros((BLK, 64), BF16)
    low = wq[:, :HALF]
    high = jnp.concatenate([wq[:, HALF:], wk[...], wv[...], zero], axis=1)
    half = jnp.where(core[...] == 0, low.astype(F32), high.astype(F32)).astype(BF16)
    tail = jnp.concatenate(
        [gain[...].astype(F32), jnp.zeros((1, HALF - BLK), F32)], axis=1
    )
    tail = jnp.concatenate([tail, jnp.zeros_like(tail)], axis=0).astype(BF16)
    block = jnp.concatenate([half, tail], axis=0)
    for b in range(NB):
        out[b] = block


def prep_kernel(own, other, shard, x, dy, e, out, xd):
    i = lax.broadcasted_iota(jnp.int32, (PADB, BLK), 0)
    j = lax.broadcasted_iota(jnp.int32, (PADB, BLK), 1)
    eye = (i == j).astype(F32).astype(BF16)
    row = lax.broadcasted_iota(jnp.int32, (PADB, WP), 0)
    mine = shard[...] == 0
    rows = 3 * FFS

    def block(v):
        tail = jnp.concatenate(
            [v[BLK : BLK + 1, :BLK].astype(F32), jnp.zeros((1, WP - BLK), F32)], axis=1
        )
        wide = dot(v[:BLK, rows:], e[...]).astype(BF16)
        return dot(eye, v[:BLK, :rows]), jnp.where(row == BLK, tail, dot(eye, wide))

    mlp_own, out_own = block(own)
    mlp_other, out_other = block(other)
    out[0:PADB, :rows] = jnp.where(mine, mlp_own, mlp_other).astype(BF16)
    out[PADB:, :rows] = jnp.where(mine, mlp_other, mlp_own).astype(BF16)
    out[0:PADB, rows:] = jnp.where(mine, out_own, out_other).astype(BF16)
    out[PADB:, rows:] = jnp.where(mine, out_other, out_own).astype(BF16)
    xd[0] = dot(x[...], e[...]).astype(BF16)
    xd[1] = dot(dy[...], e[...]).astype(BF16)


def project_kernel(xd, gain, wa, wb, core, cos, sin, send, rows):
    n1, _ = normed(xd[0].astype(F32))
    h1 = (n1 * gain[...]).astype(BF16)
    ya = dot(h1, wa[...].reshape(WP, HALF))
    yb = dot(h1, wb[...].reshape(WP, HALF))
    first = core[...] == 0
    low = jnp.where(first, ya, yb)
    high = jnp.where(first, yb, ya)
    qkv = jnp.concatenate([low, high[:, : QKV - HALF]], axis=1)
    for j in range(10):
        part = turn(qkv[:, 128 * j : 128 * j + 128], cos[...], sin[...])
        rows[:, 128 * j : 128 * j + 128] = part
    send[60:64] = jnp.zeros((4, 48, 128), BF16)
    for unit, row, col in units():
        send[unit, 32:48, :] = (
            jnp.concatenate(
                [rows[row : row + 16, col : col + D], rows[row + 16 : row + 32, col : col + D]],
                axis=1,
            ).astype(BF16)
            * 0.125
        ).astype(BF16)
    for s in range(2):
        for g in range(KH):
            both = jnp.concatenate(
                [
                    rows[s * 64 : s * 64 + 64, 960 + D * g : 960 + D * g + D],
                    qkv[s * 64 : s * 64 + 64, 1280 + D * g : 1280 + D * g + D],
                ],
                axis=1,
            ).astype(BF16)
            for u in range(6):
                send[s * 30 + g * 6 + u, 0:32, :] = both[32 * (u % 2) : 32 * (u % 2) + 32]


def hidden_kernel(x0, x1, x2, x3, gain, out):
    for k, x in enumerate((x0, x1, x2, x3)):
        n1, _ = normed(x[0].astype(F32))
        out[T * k : T * k + T, :] = (n1 * gain[...]).astype(BF16)


def low_pair(block):
    lane = lax.broadcasted_iota(jnp.int32, block.shape, 1)
    zero = jnp.zeros_like(block)
    return jnp.concatenate(
        [
            jnp.where(lane < D, block, zero),
            jnp.where(lane < D, pltpu.roll(block, D, 1), zero),
        ],
        axis=0,
    ).astype(BF16)


def high_pair(block):
    lane = lax.broadcasted_iota(jnp.int32, block.shape, 1)
    zero = jnp.zeros_like(block)
    return jnp.concatenate(
        [
            jnp.where(lane >= D, pltpu.roll(block, D, 1), zero),
            jnp.where(lane >= D, block, zero),
        ],
        axis=0,
    ).astype(BF16)


def load_pair(ref, qb, first):
    return ref[qb * 8 : qb * 8 + 8, first : first + 16, :].reshape(T, 128).astype(F32)


def unpair(cols):
    flat = cols.T
    return jnp.concatenate([flat[:T], flat[T:]], axis=1).astype(BF16).reshape(8, 16, 128)


def key_block(recv, peer, kb):
    own = recv[kb * 8 : kb * 8 + 8, 0:32, :].reshape(KB // 2, 128)
    other = peer[kb * 8 : kb * 8 + 8].reshape(KB // 2, 128)
    return jnp.concatenate([own, other], axis=0)


def masked(raw, kpos, qpos):
    return jnp.where(kpos[...] <= qpos[...], raw, MASKED)


def attend_kernel(recv, peer, kpos, qpos, send, o_out, lse_out, kv_t, scores):
    for kb in range(QB):
        kv_t[kb] = key_block(recv, peer, kb).astype(F32).T.astype(BF16)
    for qb in range(QB):
        q = low_pair(load_pair(recv, qb, 32))
        top = jnp.full((8, QN), MASKED, F32)
        for kb in range(qb + 1):
            raw = dot_t(key_block(recv, peer, kb), q)
            if kb == qb:
                raw = masked(raw, kpos, qpos)
            scores[kb] = raw
            top = jnp.maximum(top, jnp.max(raw.reshape(KB // 8, 8, QN), axis=0))
        top = jnp.max(top, axis=0, keepdims=True)
        mass = jnp.zeros((8, QN), F32)
        acc = jnp.zeros((D, QN), F32)
        for kb in range(qb + 1):
            p = jnp.exp(scores[kb] - top)
            mass = mass + jnp.sum(p.reshape(KB // 8, 8, QN), axis=0)
            acc = acc + dot(kv_t[kb, D:, :], p.astype(BF16))
        mass = jnp.sum(mass, axis=0, keepdims=True)
        acc = acc / mass
        o_out[qb] = acc
        lse_out[qb] = jnp.broadcast_to(top + jnp.log(mass), (8, QN))
        send[qb * 8 : qb * 8 + 8] = unpair(acc)


def attend_back_kernel(recv, peer, kpos, qpos, core, drecv, o_in, lse_in, send, kv_t, dkv):
    for kb in range(QB):
        kv_t[kb] = key_block(recv, peer, kb)[:, :D].astype(F32).T.astype(BF16)
    dkv[...] = jnp.zeros_like(dkv)
    for qb in range(QB):
        q = low_pair(load_pair(recv, qb, 32))
        pair = load_pair(drecv, qb, 0)
        dz = high_pair(pair)
        flat = jnp.concatenate([pair[:, :D], pair[:, D:]], axis=0)
        delta = jnp.sum(flat.T * o_in[qb], axis=0, keepdims=True)
        lse = lse_in[qb][0:1]
        acc = jnp.zeros((D, QN), F32)
        for kb in range(qb + 1):
            block = key_block(recv, peer, kb)
            raw = dot_t(block, q)
            if kb == qb:
                raw = masked(raw, kpos, qpos)
            p = jnp.exp(raw - lse)
            ds = (p * (dot_t(block, dz) - delta)).astype(BF16)
            dkv[kb] += dot(ds, q) + dot(p.astype(BF16), dz)
            acc = acc + dot(kv_t[kb], ds)
        send[qb * 8 : qb * 8 + 8, 64:80, :] = unpair(acc * 0.125)
    for kb in range(QB):
        own = dkv[kb, : KB // 2, :]
        other = dkv[kb, KB // 2 :, :]
        low = jnp.where(core[...] == 0, own, other)
        high = jnp.where(core[...] == 0, other, own)
        send[kb * 8 : kb * 8 + 8, 0:32, :] = low.astype(BF16).reshape(8, 32, 128)
        send[kb * 8 : kb * 8 + 8, 32:64, :] = high.astype(BF16).reshape(8, 32, 128)


def out_kernel(recv, xd, e, gain, w, olp_out, x1_out, h2_out, ol):
    unpack_rows(recv, ol, 0)
    olp = dot(ol[...], e[...]).astype(BF16)
    olp_out[...] = olp
    x1 = xd[0].astype(F32) + dot(olp, w[:, :, 3 * FFS :].reshape(WP, WP))
    x1_out[...] = x1
    n2, _ = normed(x1)
    h2_out[...] = (n2 * gain[...]).astype(BF16)


def mlp_kernel(h_a, h_b, dy_a, dy_b, w, back_a, back_b, act, dgate, dup):
    wg = w[:, :, 0:FFS].reshape(WP, FFS)
    wu = w[:, :, FFS : 2 * FFS].reshape(WP, FFS)
    wd = w[:, :, 2 * FFS : 3 * FFS].reshape(WP, FFS)
    for i, (h_in, dy_in, back) in enumerate(((h_a, dy_a, back_a), (h_b, dy_b, back_b))):
        h = h_in[...]
        gate = dot(h, wg)
        up = dot(h, wu)
        dact = dot(dy_in[1], wd)
        sig = jax.nn.sigmoid(gate)
        silu = gate * sig
        act[i] = (silu * up).astype(BF16)
        dg = (dact * up * sig * (1.0 + gate * (1.0 - sig))).astype(BF16)
        du = (dact * silu).astype(BF16)
        dgate[i] = dg
        dup[i] = du
        back[...] = (dot_t(dg, wg) + dot_t(du, wu)).astype(BF16)


def mlp_part_kernel(near, far, w, part, part_far):
    wd = w[:, :, 2 * FFS : 3 * FFS].reshape(WP, FFS)
    part[0] = dot_t(near[0], wd).astype(BF16)
    part[1] = dot_t(far[0], wd).astype(BF16)
    part_far[0] = dot_t(near[1], wd).astype(BF16)
    part_far[1] = dot_t(far[1], wd).astype(BF16)


def mlp_grad_kernel(
    h0, h1, h2, h3, d0, d1, d2, d3, act_n, act_f, gate_n, gate_f, up_n, up_f, out
):
    h = jnp.concatenate([h0[...], h1[...], h2[...], h3[...]], axis=0)
    d = jnp.concatenate([d0[1], d1[1], d2[1], d3[1]], axis=0)
    for k, (left, near, far) in enumerate(((h, gate_n, gate_f), (h, up_n, up_f), (d, act_n, act_f))):
        right = jnp.concatenate(
            [near[...].reshape(2 * T, FFS), far[...].reshape(2 * T, FFS)], axis=0
        )
        out[:, 32 * k : 32 * k + 32, :] = tdot(left, right).astype(BF16).reshape(NB, 32, FFS)


def mixed_kernel(own, away, x1, e, out):
    total = own[0].astype(F32) + away[...].astype(F32)
    out[...] = dot_t((x1[...] + total).astype(BF16), e[...]).astype(BF16)


def mid_back_kernel(
    b0, b1, b2, b3, x1, gain, xd, w, e, dx1_out, da_out, send, gain_part, dol
):
    dh2 = (b0[...].astype(F32) + b1[...].astype(F32)) + (
        b2[...].astype(F32) + b3[...].astype(F32)
    )
    n2, r2 = normed(x1[...])
    gain_part[...] = jnp.sum(dh2 * n2, axis=0, keepdims=True)
    dx1 = xd[1].astype(F32) + norm_back(dh2 * gain[...], n2, r2)
    dx1_out[...] = dx1
    da = dx1.astype(BF16)
    da_out[...] = dot_t(da, e[...]).astype(BF16)
    wide = dot_t(da, w[:, :, 3 * FFS :].reshape(WP, WP)).astype(BF16)
    dol[...] = dot_t(wide, e[...]).astype(BF16)
    send[60:64] = jnp.zeros((4, 16, 128), BF16)
    pack_rows(dol, send, 0)


def unpack_back_kernel(recv, cos, sin, da, slot, full, s0, s1, s2, s3, rows, held):
    unpack_rows(recv, rows, 64)
    for s in range(2):
        for g in range(KH):
            total = recv[s * 30 + g * 6, 0:64, :].astype(F32)
            for u in range(1, 6):
                total = total + recv[s * 30 + g * 6 + u, 0:64, :].astype(F32)
            rows[s * 64 : s * 64 + 64, 960 + D * g : 960 + D * g + D] = total[:, :D]
            full[s * 64 : s * 64 + 64, 1280 + D * g : 1280 + D * g + D] = total[:, D:].astype(BF16)
    for j in range(10):
        full[:, 128 * j : 128 * j + 128] = turn(
            rows[:, 128 * j : 128 * j + 128], cos[...], -sin[...]
        ).astype(BF16)
    for t in range(4):
        first = QUART * t
        inside = min(max(QKV - first, 0), QUART)
        if inside:
            held[t, :, :inside] = full[:, first : first + inside]
        if inside < QUART:
            start = first + inside - QKV
            held[t, :, inside:] = da[:, start : start + QUART - inside]
    for k, out in enumerate((s0, s1, s2, s3)):
        out[...] = held[slot[k]]


def tokens_back_kernel(full, wa, wb, core, xd, gain, dx1, e, tokens_grad, gain_part):
    low = full[:, :HALF].astype(F32)
    high = jnp.concatenate([full[:, HALF:], jnp.zeros((T, 64), BF16)], axis=1).astype(F32)
    first = core[...] == 0
    ga = jnp.where(first, low, high).astype(BF16)
    gb = jnp.where(first, high, low).astype(BF16)
    dh1 = dot_t(ga, wa[...].reshape(WP, HALF)) + dot_t(gb, wb[...].reshape(WP, HALF))
    n1, r1 = normed(xd[0].astype(F32))
    gain_part[...] = jnp.sum(dh1 * n1, axis=0, keepdims=True)
    grad = dx1[...] + norm_back(dh1 * gain[...], n1, r1)
    high_part = grad.astype(BF16)
    rest = grad - high_part.astype(F32)
    mid_part = rest.astype(BF16)
    low_part = (rest - mid_part.astype(F32)).astype(BF16)
    tokens_grad[...] = dot_t(high_part, e[...]) + (
        dot_t(mid_part, e[...]) + dot_t(low_part, e[...])
    )


def proj_grad_kernel(h1_all, o_near, o_far, g0, g1, g2, g3, edge, gains, out):
    ol = jnp.concatenate([o_near[0], o_far[0], o_near[1], o_far[1]], axis=0)
    grads = jnp.concatenate([g0[...], g1[...], g2[...], g3[...]], axis=0)
    total = jnp.where(edge[...] < QKV, tdot(h1_all[...], grads), tdot(ol, grads))
    out[...] = total.astype(BF16).reshape(NB, 32, QUART)
    out[:, 30:31, :] = gains[...]


def total_kernel(pieces, out):
    total = pieces[0].astype(F32)
    for b in range(1, NB):
        total = total + pieces[b].astype(F32)
    out[...] = total.astype(BF16)


def last_kernel(p0, p1, p2, p3, slot, wq, wk, wv, wo, gains, held):
    for k, p in enumerate((p0, p1, p2, p3)):
        held[k] = p[...].astype(F32)
    gains[...] = held[0, 30:31, :] + held[1, 30:31, :] + held[2, 30:31, :] + held[3, 30:31, :]
    full = jnp.concatenate([held[slot[q], :BLK, :] for q in range(4)], axis=1)
    wq[...] = full[:, :960]
    wk[...] = full[:, 960:1280]
    wv[...] = full[:, 1280:QKV]
    wo[...] = full[:, QKV:]


def shards(
    tokens,
    positions,
    out_grad,
    attn_gain,
    w_query,
    key_weight,
    value_weight,
    w_out,
    mlp_gain,
    w_gate,
    w_up,
    w_down,
):
    at = np.arange(WIDTH)
    block = at // BLK
    table = np.zeros((WIDTH, WP), np.float32)
    table[at, ((block % 16) * 2 + block // 16) * PADB + at % BLK] = 1.0
    spread = jnp.asarray(table, BF16)
    tensor = lax.axis_index("tensor")
    core = (tensor % 2).reshape(1, 1).astype(jnp.int32)

    (w1_send,) = call(
        first_kernel, [((NB, PADB, HALF), BF16)],
        w_query, key_weight, value_weight, attn_gain.reshape(1, BLK), core,
    )
    rows = jnp.concatenate([w_gate, w_up, w_down.T, w_out], axis=1)
    gain_row = jnp.pad(mlp_gain[None, :], ((0, 0), (0, rows.shape[1] - BLK)))
    rows = jnp.concatenate([rows, gain_row], axis=0)
    other = swap(rows, "shard", 1)
    rows, other, w1_send = lax.optimization_barrier((rows, other, w1_send))
    w1a = exchange(w1_send, CS)
    shard = lax.axis_index("shard").reshape(1, 1).astype(jnp.int32)
    pair, xd = call(
        prep_kernel,
        [((2 * PADB, 3 * FFS + WP), BF16), ((2, T, WP), BF16)],
        rows, other, shard, tokens.reshape(T, WIDTH), out_grad.reshape(T, WIDTH), spread,
    )

    half = D // 2
    freq = ROPE_BASE ** (-2.0 * jnp.arange(half, dtype=F32) / D)
    theta = positions.reshape(T).astype(F32)[:, None] * freq
    c, s = jnp.cos(theta), jnp.sin(theta)
    cos = jnp.concatenate([c, c, c, c], axis=1)
    sin = jnp.concatenate([-s, s, -s, s], axis=1)

    early = pair
    w1a, pair, xd, cos, sin = lax.optimization_barrier((w1a, pair, xd, cos, sin))
    w1b = swap(w1a, "tensor", 1)
    w2 = lax.all_gather(early, "context", axis=0, tiled=True).reshape(NB, PADB, -1)
    gain2 = w2[:, 30, 3 * FFS : 3 * FFS + PADB].reshape(1, WP).astype(F32)
    gain1 = w1a[:, 30, :PADB].reshape(1, WP).astype(F32)

    (send,) = call(
        project_kernel,
        [((64, 48, 128), BF16)],
        xd, gain1, w1a, w1b, core, cos, sin,
        scratch=[pltpu.VMEM((T, 1280), F32)],
    )
    recv = exchange(send, CT)
    peer = swap(recv[:, :32, :], "tensor", 1)
    row = jnp.arange(KB, dtype=jnp.int32)
    kpos = (
        64 * ((row % (KB // 2)) // 32)
        + 32 * jnp.bitwise_xor(tensor % 2, row // (KB // 2))
        + row % 32
    ).reshape(KB, 1)

    lane = jnp.arange(QN, dtype=jnp.int32)
    qpos = (
        64 * ((lane % T) // 16)
        + 32 * (lax.axis_index("tensor") % 2)
        + 16 * (lane // T)
        + lane % 16
    ).reshape(1, QN)
    o_send, o_cols, lse = call(
        attend_kernel,
        [((64, 16, 128), BF16), ((QB, D, QN), F32), ((QB, 8, QN), F32)],
        recv, peer, kpos, qpos,
        scratch=[pltpu.VMEM((QB, 128, KB), BF16), pltpu.VMEM((QB, KB, QN), F32)],
    )
    o_recv = exchange(o_send, CT)
    xd, o_send = lax.optimization_barrier((xd, o_send))
    xd_one, xd_two = swap(xd, "tensor", 1), swap(xd, "tensor", 2)

    olp, x1, h2 = call(
        out_kernel,
        [((T, WP), BF16), ((T, WP), F32), ((T, WP), BF16)],
        o_recv, xd, spread, gain2, w2,
        scratch=[pltpu.VMEM((T, WIDTH), BF16)],
    )
    h2, xd_two = lax.optimization_barrier((h2, xd_two))
    xd_three = swap(xd_two, "tensor", 1)
    h2_one, h2_two, h2_three = (swap(h2, "tensor", k) for k in (1, 2, 3))
    tiles = [((T, WP), BF16)] * 2 + [((2, T, FFS), BF16)] * 3
    back0, back1, act_n, gate_n, up_n = call(
        mlp_kernel, tiles, h2, h2_one, xd, xd_one, w2
    )
    h2_two, h2_three, back1 = lax.optimization_barrier((h2_two, h2_three, back1))
    back2, back3, act_f, gate_f, up_f = call(
        mlp_kernel, tiles, h2_two, h2_three, xd_two, xd_three, w2
    )
    back1, back2, back3 = (swap(b, "tensor", k + 1) for k, b in enumerate((back1, back2, back3)))
    (mlp_grad,) = call(
        mlp_grad_kernel, [((NB, 96, FFS), BF16)],
        h2, h2_one, h2_two, h2_three, xd, xd_one, xd_two, xd_three,
        act_n, act_f, gate_n, gate_f, up_n, up_f,
    )
    part, part_far = call(mlp_part_kernel, [((2, T, WP), BF16)] * 2, act_n, act_f, w2)
    back1, back2, back3, mlp_grad, part, part_far = lax.optimization_barrier(
        (back1, back2, back3, mlp_grad, part, part_far)
    )
    mlp_part = scattered(mlp_grad)

    dx1, da, d_send, gain2_part = call(
        mid_back_kernel,
        [((T, WP), F32), ((T, WIDTH), BF16), ((64, 16, 128), BF16), ((1, WP), F32)],
        back0, back1, back2, back3, x1, gain2, xd, w2, spread,
        scratch=[pltpu.VMEM((T, WIDTH), BF16)],
    )
    d_recv = exchange(d_send, CT)
    part_far, olp, d_send = lax.optimization_barrier((part_far, olp, d_send))
    part = part.astype(F32) + swap(part_far, "tensor", 1).astype(F32)
    part = part.astype(BF16)
    d_recv, part = lax.optimization_barrier((d_recv, part))
    part_away = swap(part[1], "tensor", 2)
    ol_near = from_pair(olp)
    (back_send,) = call(
        attend_back_kernel,
        [((64, 80, 128), BF16)],
        recv, peer, kpos, qpos, core, d_recv, o_cols, lse,
        scratch=[pltpu.VMEM((QB, D, KB), BF16), pltpu.VMEM((QB, KB, 128), F32)],
    )
    back_send, part_away, ol_near = lax.optimization_barrier((back_send, part_away, ol_near))
    ol_far = swap(ol_near, "tensor", 1)
    back_recv = exchange(back_send, CT)
    (mixed,) = call(mixed_kernel, [((T, WIDTH), BF16)], part, part_away, x1, spread)
    (h1_all,) = call(
        hidden_kernel, [((4 * T, WP), BF16)], xd, xd_one, xd_two, xd_three, gain1
    )
    back_recv, mixed, h1_all = lax.optimization_barrier((back_recv, mixed, h1_all))

    slot = jnp.bitwise_xor(tensor, jnp.arange(4, dtype=jnp.int32))
    full, *dq_send = call(
        unpack_back_kernel,
        [((T, QKV), BF16)] + [((T, QUART), BF16)] * 4,
        back_recv, cos, sin, da, slot,
        specs={4: pl.BlockSpec(memory_space=pltpu.SMEM)},
        scratch=[pltpu.VMEM((T, 1280), F32), pltpu.VMEM((4, T, QUART), BF16)],
    )
    dq_recv = from_each(dq_send)
    tokens_grad, gain1_part = call(
        tokens_back_kernel,
        [((T, WIDTH), F32), ((1, WP), F32)],
        full, w1a, w1b, core, xd, gain1, dx1, spread,
    )
    gains = jnp.concatenate(
        [gain1_part.reshape(NB, PADB), gain2_part.reshape(NB, PADB)], axis=1
    ).astype(BF16)
    gains = jnp.pad(gains, ((0, 0), (0, QUART - 2 * PADB))).reshape(NB, 1, QUART)
    edge = (tensor * QUART + jnp.arange(QUART, dtype=jnp.int32)).reshape(1, QUART)
    (proj_grad,) = call(
        proj_grad_kernel, [((NB, 32, QUART), BF16)],
        h1_all, ol_near, ol_far, *dq_recv, edge, gains,
    )
    proj_recv = exchange(proj_grad, CS)
    mlp_part, proj_grad = lax.optimization_barrier((mlp_part, proj_grad))
    mlp_sum = over_shard(mlp_part)
    proj_recv, mlp_sum = lax.optimization_barrier((proj_recv, mlp_sum))
    (proj_sum,) = call(total_kernel, [((32, QUART), BF16)], proj_recv)
    wq_grad, wk_grad, wv_grad, wo_grad, gain_sums = call(
        last_kernel,
        [((BLK, 960), F32), ((BLK, 320), F32), ((BLK, 320), F32), ((BLK, 960), F32), ((1, QUART), F32)],
        *from_each([proj_sum] * 4), slot,
        specs={4: pl.BlockSpec(memory_space=pltpu.SMEM)},
        scratch=[pltpu.VMEM((4, 32, QUART), F32)],
    )
    gain_sums = gain_sums[0]
    return (
        mixed.reshape(tokens.shape),
        tokens_grad.reshape(tokens.shape),
        gain_sums[:BLK],
        wq_grad,
        wk_grad,
        wv_grad,
        wo_grad,
        gain_sums[PADB : PADB + BLK],
        mlp_sum[:BLK],
        mlp_sum[32 : 32 + BLK],
        mlp_sum[64 : 64 + BLK].T,
    )


def solution(mesh):
    tok = P("shard", ("context", "tensor"), None)
    vec = P(SC)
    row = P(SC, None)
    wide = P(SC, "tensor")
    return jax.shard_map(
        shards,
        mesh=mesh,
        in_specs=(
            tok, P("shard", ("context", "tensor")), tok,
            vec, row, row, row, row, vec, wide, wide, P("tensor", SC),
        ),
        out_specs=(
            tok, tok, vec, row, row, row, row, vec, wide, wide, P("tensor", SC),
        ),
        check_vma=False,
    )
```
